256 devices in a mesh: row: 8 (over x, core), col: 32 (over z, y).
Axes of the slice: x: 4, y: 4, z: 8, core: 2. Of those that a mesh axis runs over, the one named last changes fastest.
Arguments:
- matrix: bfloat16 [16384, 65536], P('row', 'col'), may hold values from -8 to 8
- basis: bfloat16 [16384, 256], P(('row', 'col')), may hold values from -110 to 110
Outputs:
- orthobasis: float32 [16384, 256], P(('row', 'col'))
- triangle: float32 [256, 256], replicated
The draws below stay inside these ranges and needn't reach their ends.
All inputs are finite; a program needn't handle non-finite values.
Results may differ from the reference program's by a relative error of at most 0.0018.
Values may be sent and summed in bfloat16 or wider, within the bound.
A program may use at most 64 MiB of HBM per device.

```python
import jax
import jax.numpy as jnp
from jax import lax

N = 65536
K = 256
ROWS = 16384


def draw_matrix(key, part):
    key = jax.random.fold_in(key, 11)
    first, second = jax.random.split(key)
    trend = 0.5 + jnp.arange(ROWS, dtype=jnp.float32) / ROWS
    rough = jax.random.uniform(first, (ROWS,), jnp.float32, 0.8, 1.25)
    noise = jnp.clip(jax.random.normal(second, (ROWS, N), jnp.float32), -4.0, 4.0)
    return (noise * (trend * rough)[:, None]).astype(jnp.bfloat16)


def draw_basis(key, part):
    key = jax.random.fold_in(key, 29)
    keys = jax.random.split(key, 4)
    scales = jnp.exp(jax.random.uniform(keys[0], (K,), jnp.float32, 0.0, jnp.log(10.0)))
    noise = jnp.clip(jax.random.normal(keys[1], (ROWS, K), jnp.float32), -4.0, 4.0)
    left = jnp.clip(jax.random.normal(keys[2], (ROWS,), jnp.float32), -3.0, 3.0)
    right = jnp.clip(jax.random.normal(keys[3], (K,), jnp.float32), -3.0, 3.0)
    common = 0.7
    values = (noise + common * left[:, None] * right[None, :]) * scales[None, :]
    return values.astype(jnp.bfloat16)


def setup_inputs(seed: int = 0) -> dict:
    streams_of = jax.random.split(jax.random.key(seed), 3)
    return {
        "matrix": draw_matrix(jax.random.fold_in(streams_of[2], 71), 0),
        "basis": draw_basis(jax.random.fold_in(streams_of[2], 71), 0),
    }


def reference(matrix, basis):
    partial_value = lax.dot_general(matrix.astype(jnp.float32), basis.astype(jnp.float32), (((0,), (0,)), ((), ())), preferred_element_type=jnp.float32)
    sketch = (partial_value * ROWS ** (-0.5)).astype(jnp.bfloat16)
    image = jnp.dot(matrix.astype(jnp.float32), sketch.astype(jnp.float32), preferred_element_type=jnp.float32) * N ** (-0.5)
    gram = jnp.dot(image.T, image, precision=lax.Precision.HIGHEST) / ROWS
    lower = jnp.linalg.cholesky(gram)
    orthobasis = jax.scipy.linalg.solve_triangular(lower, image.T, lower=True).T
    return (orthobasis, lower.T)
```

```python
import functools

import jax
import jax.numpy as jnp
from jax import lax
from jax.experimental import pallas as pl
from jax.experimental.pallas import tpu as pltpu
from jax.sharding import PartitionSpec as P

F32 = jnp.float32
BF16 = jnp.bfloat16
NX, NY, NZ = 4, 4, 8
KC = 256
BLK = 64
GA = 48
IA = 48
IDT = BF16
XS = (2, 1, 3, 0)


def kernel(
    a_hbm, basis, img_out, gram_out,
    av, g, bt, part, rk, own, xs, xr, st, im, sa, sb, ya, zb, ta, ub, za, yb,
    g0, gk, g1, gx, g2, gy, gz, gf,
    asem, s_gz, r_gz, s_gzy, r_gzy, s_gy, r_gy, s_gyz, r_gyz,
    s_k, r_k, s_x, r_x, s_sx, r_sx, s_sk, r_sk,
    s_ya, r_ya, s_zb, r_zb, s_za, r_za, s_yb, r_yb,
    s_q, r_q,
):
    r = lax.axis_index("row")
    c = lax.axis_index("col")
    x, k = r // 2, r % 2
    z, y = c // NY, c % NY

    def at_x(s):
        return (((x + s) % NX) * 2 + k, c)

    def at_k():
        return (x * 2 + 1 - k, c)

    def at_y(s):
        return (r, z * NY + (y + s) % NY)

    def at_z(s):
        return (r, ((z + s) % NZ) * NY + y)

    loads = []
    for j in range(8):
        cp = pltpu.make_async_copy(a_hbm.at[:, pl.ds(256 * j, 256)], av.at[j], asem.at[j])
        cp.start()
        loads.append(cp)

    barrier = pltpu.get_barrier_semaphore()
    for s in range(1, NZ):
        pl.semaphore_signal(barrier, 1, device_id=at_z(s))
    for s in range(1, NY):
        pl.semaphore_signal(barrier, 1, device_id=at_y(s))
    for s in range(1, NX):
        pl.semaphore_signal(barrier, 1, device_id=at_x(s))
    pl.semaphore_signal(barrier, 1, device_id=at_k())
    g[z, y] = basis[...]
    pl.semaphore_wait(barrier, NZ + NY + NX - 3 + 1)

    sends = []

    def copy(src, dst, ss, rs, dev):
        cp = pltpu.make_async_remote_copy(src, dst, ss, rs, device_id=dev)
        cp.start()
        sends.append(cp)
        return cp

    hi, lo = pl.ds(0, GA), pl.ds(GA, BLK - GA)
    zorder = (1, 7, 2, 6, 3, 5, 4)
    cy = {s: copy(basis.at[lo], g.at[z, y, lo], s_gy.at[s], r_gy.at[s], at_y(s)) for s in (2, 1, 3)}
    cz = {s: copy(basis.at[hi], g.at[z, y, hi], s_gz.at[s], r_gz.at[s], at_z(s)) for s in zorder}
    czy = {}
    for t in (2, 1, 3):
        czy[0, t] = copy(basis.at[hi], g.at[z, y, hi], s_gzy.at[0, t], r_gzy.at[0, t], at_y(t))
    for s in (1, 3, 2):
        cy[s].wait_recv()
    cyz = {}
    for s in (4, 3, 5, 2, 6, 1, 7):
        cyz[s] = copy(g.at[z, :, lo], g.at[z, :, lo], s_gyz.at[s], r_gyz.at[s], at_z(s))
    for s in zorder:
        cz[s].wait_recv()
        zs = (z + NZ - s) % NZ
        for t in (2, 1, 3):
            czy[s, t] = copy(
                g.at[zs, y, hi], g.at[zs, y, hi], s_gzy.at[s, t], r_gzy.at[s, t], at_y(t)
            )
    for cp in cyz.values():
        cp.wait_recv()
    for cp in czy.values():
        cp.wait_recv()

    def turn(i, carry):
        bt[:, pl.ds(pl.multiple_of(i * 256, 256), 256)] = g[i].reshape(NY * BLK, KC).T
        return carry

    lax.fori_loop(0, NZ, turn, 0)
    for cp in loads:
        cp.wait()

    def product(j):
        return jnp.dot(bt[...], av[j], preferred_element_type=F32)

    ck = []
    for i, s in enumerate(XS):
        part[i] = product(2 * ((x + s) % NX) + 1 - k)
        ck.append(copy(part.at[i], rk.at[i], s_k.at[i], r_k.at[i], at_k()))
    cx = []
    for i, s in enumerate(XS):
        p = product(2 * ((x + s) % NX) + k)
        ck[i].wait_recv()
        p = p + rk[i]
        if s:
            xs[i] = p
            cx.append(copy(xs.at[i], xr.at[i], s_x.at[i], r_x.at[i], at_x(s)))
        else:
            own[...] = p
    for cp in cx:
        cp.wait_recv()
    total = (own[...] + xr[0]) + (xr[1] + xr[2])
    st[r] = (total * (16384.0**-0.5)).astype(BF16)
    csx = {}
    csk = {0: copy(st.at[r], st.at[r], s_sk.at[0], r_sk.at[0], at_k())}
    for s in (2, 1, 3):
        csx[s] = copy(st.at[r], st.at[r], s_sx.at[s], r_sx.at[s], at_x(s))

    def add(ja, jb, first, last):
        def tile(i, carry):
            zi = i
            rows = pl.ds(pl.multiple_of(i * 256, 256), 256)
            v = lax.dot_general(av[ja, rows, :], st[ja], (((1,), (1,)), ((), ())), preferred_element_type=F32)
            v += lax.dot_general(av[jb, rows, :], st[jb], (((1,), (1,)), ((), ())), preferred_element_type=F32)
            if not first:
                v += im[rows, :]
            im[rows, :] = v
            return carry

        lax.fori_loop(0, 8, tile, 0)

    csk[0].wait_recv()
    add(r, x * 2 + 1 - k, True, False)
    for s in (1, 3, 2):
        csx[s].wait_recv()
        xq = (x + NX - s) % NX
        j = 2 * xq + k
        csk[s] = copy(st.at[j], st.at[j], s_sk.at[s], r_sk.at[s], at_k())
    for s in (1, 3, 2):
        csk[s].wait_recv()
        xq = (x + NX - s) % NX
        add(2 * xq + k, 2 * xq + 1 - k, False, s == 2)

    nb = BLK - IA
    v4 = im.reshape(NZ, NY, BLK, KC)
    cya, czb = {}, {}
    for s in (2, 1, 3):
        yq = (y + s) % NY
        sa[s] = v4[:, yq, :IA, :].astype(IDT)
        cya[s] = copy(sa.at[s], ya.at[s], s_ya.at[s], r_ya.at[s], at_y(s))
    for s in (4, 3, 5, 2, 6, 1, 7):
        zq = (z + s) % NZ
        sb[s] = v4[zq, :, IA:, :].astype(IDT)
        czb[s] = copy(sb.at[s], zb.at[s], s_zb.at[s], r_zb.at[s], at_z(s))
    ta[...] = v4[:, y, :IA, :]
    for s in (1, 3, 2):
        cya[s].wait_recv()
    ta[...] = (ta[...] + ya[1].astype(F32)) + (ya[2].astype(F32) + ya[3].astype(F32))
    cza = {}
    for s in (4, 3, 5, 2, 6, 1, 7):
        cza[s] = copy(ta.at[(z + s) % NZ], za.at[s], s_za.at[s], r_za.at[s], at_z(s))
    u = v4[z, :, IA:, :]
    for s in (1, 7, 2, 6, 3, 5, 4):
        czb[s].wait_recv()
        u = u + zb[s].astype(F32)
    ub[...] = u
    cyb = {}
    for s in (2, 1, 3):
        cyb[s] = copy(ub.at[(y + s) % NY], yb.at[s], s_yb.at[s], r_yb.at[s], at_y(s))
    low = ub[y]
    for s in (1, 3, 2):
        cyb[s].wait_recv()
        low = low + yb[s]
    high = ta[z]
    for s in (1, 7, 2, 6, 3, 5, 4):
        cza[s].wait_recv()
        high = high + za[s]
    scale = 65536.0**-0.5
    img_out[:IA, :] = high * scale
    img_out[IA:, :] = low * scale

    img = img_out[...]
    g0[...] = lax.dot_general(
        img, img, (((0,), (0,)), ((), ())),
        precision=lax.Precision.HIGHEST, preferred_element_type=F32,
    ) * (1.0 / 16384.0)
    half = pl.ds(pl.multiple_of(128 * k, 128), 128)
    other = pl.ds(pl.multiple_of(128 * (1 - k), 128), 128)
    cp = copy(g0.at[other], gk, s_q.at[0], r_q.at[0], at_k())
    cp.wait_recv()
    g1[...] = g0[half, :] + gk[...]
    cps = []
    for s in (2, 1, 3):
        piece = pl.ds(pl.multiple_of(32 * ((x + s) % NX), 32), 32)
        cps.append(copy(g1.at[piece], gx.at[s - 1], s_q.at[s], r_q.at[s], at_x(s)))
    for cp in cps:
        cp.wait_recv()
    g2[...] = (g1[pl.ds(pl.multiple_of(32 * x, 32), 32), :] + gx[0]) + (gx[1] + gx[2])
    cps = []
    for s in (2, 1, 3):
        piece = pl.ds(pl.multiple_of(8 * ((y + s) % NY), 8), 8)
        cps.append(copy(g2.at[piece], gy.at[s - 1], s_q.at[3 + s], r_q.at[3 + s], at_y(s)))
    for cp in cps:
        cp.wait_recv()
    gz[z] = (g2[pl.ds(pl.multiple_of(8 * y, 8), 8), :] + gy[0]) + (gy[1] + gy[2])
    cps = []
    for s in (4, 3, 5, 2, 6, 1, 7):
        cps.append(copy(gz.at[z], gz.at[z], s_q.at[6 + s], r_q.at[6 + s], at_z(s)))
    for cp in cps:
        cp.wait_recv()
    row8 = pl.ds(pl.multiple_of(128 * k + 32 * x + 8 * y, 8), 8)
    row32 = pl.ds(pl.multiple_of(128 * k + 32 * x, 32), 32)
    gf[row8, :] = ((gz[0] + gz[1]) + (gz[2] + gz[3])) + ((gz[4] + gz[5]) + (gz[6] + gz[7]))
    cps = []
    for s in (2, 1, 3):
        cps.append(copy(gf.at[row8], gf.at[row8], s_q.at[13 + s], r_q.at[13 + s], at_y(s)))
    for cp in cps:
        cp.wait_recv()
    cps = []
    for s in (2, 1, 3):
        cps.append(copy(gf.at[row32], gf.at[row32], s_q.at[16 + s], r_q.at[16 + s], at_x(s)))
    for cp in cps:
        cp.wait_recv()
    cp = copy(gf.at[half], gf.at[half], s_q.at[20], r_q.at[20], at_k())
    cp.wait_recv()
    gram_out[...] = gf[...]
    for cp in sends:
        cp.wait_send()


def image_and_gram(matrix, basis):
    dma = pltpu.SemaphoreType.DMA
    nb = BLK - IA
    sems = []
    for shape in (
        (NZ,), (NZ, NY), (NY,), (NZ,),
        (4,), (4,), (4,), (4,),
        (NY,), (NZ,), (NZ,), (NY,), (21,),
    ):
        sems += [dma(shape), dma(shape)]
    return pl.pallas_call(
        kernel,
        out_shape=(
            jax.ShapeDtypeStruct((BLK, KC), F32),
            jax.ShapeDtypeStruct((KC, KC), F32),
        ),
        in_specs=[pl.BlockSpec(memory_space=pl.ANY), pl.BlockSpec(memory_space=pltpu.VMEM)],
        out_specs=(pl.BlockSpec(memory_space=pltpu.VMEM), pl.BlockSpec(memory_space=pltpu.VMEM)),
        scratch_shapes=[
            pltpu.VMEM((8, 2048, 256), BF16),
            pltpu.VMEM((NZ, NY, BLK, KC), BF16),
            pltpu.VMEM((KC, 2048), BF16),
            pltpu.VMEM((4, KC, 256), F32),
            pltpu.VMEM((4, KC, 256), F32),
            pltpu.VMEM((KC, 256), F32),
            pltpu.VMEM((3, KC, 256), F32),
            pltpu.VMEM((3, KC, 256), F32),
            pltpu.VMEM((8, KC, 256), BF16),
            pltpu.VMEM((2048, KC), F32),
            pltpu.VMEM((NY, NZ, IA, KC), IDT),
            pltpu.VMEM((NZ, NY, nb, KC), IDT),
            pltpu.VMEM((NY, NZ, IA, KC), IDT),
            pltpu.VMEM((NZ, NY, nb, KC), IDT),
            pltpu.VMEM((NZ, IA, KC), F32),
            pltpu.VMEM((NY, nb, KC), F32),
            pltpu.VMEM((NZ, IA, KC), F32),
            pltpu.VMEM((NY, nb, KC), F32),
            pltpu.VMEM((KC, KC), F32),
            pltpu.VMEM((128, KC), F32),
            pltpu.VMEM((128, KC), F32),
            pltpu.VMEM((3, 32, KC), F32),
            pltpu.VMEM((32, KC), F32),
            pltpu.VMEM((3, 8, KC), F32),
            pltpu.VMEM((NZ, 8, KC), F32),
            pltpu.VMEM((KC, KC), F32),
            dma((8,)),
            *sems,
        ],
        compiler_params=pltpu.CompilerParams(
            collective_id=0, has_side_effects=True, vmem_limit_bytes=48 * 2**20
        ),
        cost_estimate=pl.CostEstimate(flops=2**33, bytes_accessed=2**23, transcendentals=0),
        name="image_and_gram",
    )(matrix, basis)


def body(matrix, basis):
    image, gram = image_and_gram(matrix, basis)
    lower = jnp.linalg.cholesky(gram)
    orthobasis = jax.scipy.linalg.solve_triangular(lower, image.T, lower=True).T
    return (orthobasis, lower.T)


def solution(mesh):
    in_specs = (P("row", "col"), P(("row", "col"), None))
    out_specs = (P(("row", "col"), None), P())
    return jax.shard_map(body, mesh=mesh, in_specs=in_specs, out_specs=out_specs, check_vma=False)
```

```python
import functools

import jax
import jax.numpy as jnp
from jax import lax
from jax.experimental import pallas as pl
from jax.experimental.pallas import tpu as pltpu
from jax.sharding import PartitionSpec as P

F32 = jnp.float32
BF16 = jnp.bfloat16
NX, NY, NZ = 4, 4, 8
KC = 256
BLK = 64
GA = 48
IA = 48
IDT = BF16
XS = (2, 1, 3, 0)


def kernel(
    a_hbm, basis, img_out, gram_out,
    av, g, bt, part, rk, own, xs, xr, st, im, sa, sb, ya, zb, ta, ub, za, yb,
    g0, gk, g1, gx, g2, gy, gz, gf,
    asem, s_gz, r_gz, s_gzy, r_gzy, s_gy, r_gy, s_gyz, r_gyz,
    s_k, r_k, s_x, r_x, s_sx, r_sx, s_sk, r_sk,
    s_ya, r_ya, s_zb, r_zb, s_za, r_za, s_yb, r_yb,
    s_q, r_q,
):
    r = lax.axis_index("row")
    c = lax.axis_index("col")
    x, k = r // 2, r % 2
    z, y = c // NY, c % NY

    def at_x(s):
        return (((x + s) % NX) * 2 + k, c)

    def at_k():
        return (x * 2 + 1 - k, c)

    def at_y(s):
        return (r, z * NY + (y + s) % NY)

    def at_z(s):
        return (r, ((z + s) % NZ) * NY + y)

    loads = []
    for j in range(8):
        cp = pltpu.make_async_copy(a_hbm.at[:, pl.ds(256 * j, 256)], av.at[j], asem.at[j])
        cp.start()
        loads.append(cp)

    barrier = pltpu.get_barrier_semaphore()
    for s in range(1, NZ):
        pl.semaphore_signal(barrier, 1, device_id=at_z(s))
    for s in range(1, NY):
        pl.semaphore_signal(barrier, 1, device_id=at_y(s))
    for s in range(1, NX):
        pl.semaphore_signal(barrier, 1, device_id=at_x(s))
    pl.semaphore_signal(barrier, 1, device_id=at_k())
    g[z, y] = basis[...]
    pl.semaphore_wait(barrier, NZ + NY + NX - 3 + 1)

    sends = []

    def copy(src, dst, ss, rs, dev):
        cp = pltpu.make_async_remote_copy(src, dst, ss, rs, device_id=dev)
        cp.start()
        sends.append(cp)
        return cp

    hi, lo = pl.ds(0, GA), pl.ds(GA, BLK - GA)
    zorder = (1, 7, 2, 6, 3, 5, 4)
    cy = {s: copy(basis.at[lo], g.at[z, y, lo], s_gy.at[s], r_gy.at[s], at_y(s)) for s in (2, 1, 3)}
    cz = {s: copy(basis.at[hi], g.at[z, y, hi], s_gz.at[s], r_gz.at[s], at_z(s)) for s in zorder}
    czy = {}
    for t in (2, 1, 3):
        czy[0, t] = copy(basis.at[hi], g.at[z, y, hi], s_gzy.at[0, t], r_gzy.at[0, t], at_y(t))
    for s in (1, 3, 2):
        cy[s].wait_recv()
    cyz = {}
    for s in (4, 3, 5, 2, 6, 1, 7):
        cyz[s] = copy(g.at[z, :, lo], g.at[z, :, lo], s_gyz.at[s], r_gyz.at[s], at_z(s))
    for s in zorder:
        cz[s].wait_recv()
        zs = (z + NZ - s) % NZ
        for t in (2, 1, 3):
            czy[s, t] = copy(
                g.at[zs, y, hi], g.at[zs, y, hi], s_gzy.at[s, t], r_gzy.at[s, t], at_y(t)
            )
    for cp in cyz.values():
        cp.wait_recv()
    for cp in czy.values():
        cp.wait_recv()

    def turn(i, carry):
        bt[:, pl.ds(pl.multiple_of(i * 256, 256), 256)] = g[i].reshape(NY * BLK, KC).T
        return carry

    lax.fori_loop(0, NZ, turn, 0)
    for cp in loads:
        cp.wait()

    def product(j):
        return jnp.dot(bt[...], av[j], preferred_element_type=F32)

    ck = []
    for i, s in enumerate(XS):
        part[i] = product(2 * ((x + s) % NX) + 1 - k)
        ck.append(copy(part.at[i], rk.at[i], s_k.at[i], r_k.at[i], at_k()))
    cx = []
    for i, s in enumerate(XS):
        p = product(2 * ((x + s) % NX) + k)
        ck[i].wait_recv()
        p = p + rk[i]
        if s:
            xs[i] = p
            cx.append(copy(xs.at[i], xr.at[i], s_x.at[i], r_x.at[i], at_x(s)))
        else:
            own[...] = p
    for cp in cx:
        cp.wait_recv()
    total = (own[...] + xr[0]) + (xr[1] + xr[2])
    st[r] = (total * (16384.0**-0.5)).astype(BF16)
    csx = {}
    csk = {0: copy(st.at[r], st.at[r], s_sk.at[0], r_sk.at[0], at_k())}
    for s in (2, 1, 3):
        csx[s] = copy(st.at[r], st.at[r], s_sx.at[s], r_sx.at[s], at_x(s))

    def add(ja, jb, first, last):
        def tile(i, carry):
            zi = i
            rows = pl.ds(pl.multiple_of(i * 256, 256), 256)
            v = lax.dot_general(av[ja, rows, :], st[ja], (((1,), (1,)), ((), ())), preferred_element_type=F32)
            v += lax.dot_general(av[jb, rows, :], st[jb], (((1,), (1,)), ((), ())), preferred_element_type=F32)
            if not first:
                v += im[rows, :]
            im[rows, :] = v
            return carry

        lax.fori_loop(0, 8, tile, 0)

    csk[0].wait_recv()
    add(r, x * 2 + 1 - k, True, False)
    for s in (1, 3, 2):
        csx[s].wait_recv()
        xq = (x + NX - s) % NX
        j = 2 * xq + k
        csk[s] = copy(st.at[j], st.at[j], s_sk.at[s], r_sk.at[s], at_k())
    for s in (1, 3, 2):
        csk[s].wait_recv()
        xq = (x + NX - s) % NX
        add(2 * xq + k, 2 * xq + 1 - k, False, s == 2)

    nb = BLK - IA
    v4 = im.reshape(NZ, NY, BLK, KC)
    cya, czb = {}, {}
    for s in (2, 1, 3):
        yq = (y + s) % NY
        sa[s] = v4[:, yq, :IA, :].astype(IDT)
        cya[s] = copy(sa.at[s], ya.at[s], s_ya.at[s], r_ya.at[s], at_y(s))
    for s in (4, 3, 5, 2, 6, 1, 7):
        zq = (z + s) % NZ
        sb[s] = v4[zq, :, IA:, :].astype(IDT)
        czb[s] = copy(sb.at[s], zb.at[s], s_zb.at[s], r_zb.at[s], at_z(s))
    ta[...] = v4[:, y, :IA, :]
    for s in (1, 3, 2):
        cya[s].wait_recv()
    ta[...] = (ta[...] + ya[1].astype(F32)) + (ya[2].astype(F32) + ya[3].astype(F32))
    cza = {}
    for s in (4, 3, 5, 2, 6, 1, 7):
        cza[s] = copy(ta.at[(z + s) % NZ], za.at[s], s_za.at[s], r_za.at[s], at_z(s))
    u = v4[z, :, IA:, :]
    for s in (1, 7, 2, 6, 3, 5, 4):
        czb[s].wait_recv()
        u = u + zb[s].astype(F32)
    ub[...] = u
    cyb = {}
    for s in (2, 1, 3):
        cyb[s] = copy(ub.at[(y + s) % NY], yb.at[s], s_yb.at[s], r_yb.at[s], at_y(s))
    low = ub[y]
    for s in (1, 3, 2):
        cyb[s].wait_recv()
        low = low + yb[s]
    high = ta[z]
    for s in (1, 7, 2, 6, 3, 5, 4):
        cza[s].wait_recv()
        high = high + za[s]
    scale = 65536.0**-0.5
    img_out[:IA, :] = high * scale
    img_out[IA:, :] = low * scale

    img = img_out[...]
    g0[...] = lax.dot_general(
        img, img, (((0,), (0,)), ((), ())),
        precision=lax.Precision.HIGHEST, preferred_element_type=F32,
    ) * (1.0 / 16384.0)
    half = pl.ds(pl.multiple_of(128 * k, 128), 128)
    other = pl.ds(pl.multiple_of(128 * (1 - k), 128), 128)
    cp = copy(g0.at[other], gk, s_q.at[0], r_q.at[0], at_k())
    cp.wait_recv()
    g1[...] = g0[half, :] + gk[...]
    cps = []
    for s in (2, 1, 3):
        piece = pl.ds(pl.multiple_of(32 * ((x + s) % NX), 32), 32)
        cps.append(copy(g1.at[piece], gx.at[s - 1], s_q.at[s], r_q.at[s], at_x(s)))
    for cp in cps:
        cp.wait_recv()
    g2[...] = (g1[pl.ds(pl.multiple_of(32 * x, 32), 32), :] + gx[0]) + (gx[1] + gx[2])
    cps = []
    for s in (2, 1, 3):
        piece = pl.ds(pl.multiple_of(8 * ((y + s) % NY), 8), 8)
        cps.append(copy(g2.at[piece], gy.at[s - 1], s_q.at[3 + s], r_q.at[3 + s], at_y(s)))
    for cp in cps:
        cp.wait_recv()
    gz[z] = (g2[pl.ds(pl.multiple_of(8 * y, 8), 8), :] + gy[0]) + (gy[1] + gy[2])
    cps = []
    for s in (4, 3, 5, 2, 6, 1, 7):
        cps.append(copy(gz.at[z], gz.at[z], s_q.at[6 + s], r_q.at[6 + s], at_z(s)))
    for cp in cps:
        cp.wait_recv()
    row8 = pl.ds(pl.multiple_of(128 * k + 32 * x + 8 * y, 8), 8)
    row32 = pl.ds(pl.multiple_of(128 * k + 32 * x, 32), 32)
    gf[row8, :] = ((gz[0] + gz[1]) + (gz[2] + gz[3])) + ((gz[4] + gz[5]) + (gz[6] + gz[7]))
    cps = []
    for s in (2, 1, 3):
        cps.append(copy(gf.at[row8], gf.at[row8], s_q.at[13 + s], r_q.at[13 + s], at_y(s)))
    for cp in cps:
        cp.wait_recv()
    cps = []
    for s in (2, 1, 3):
        cps.append(copy(gf.at[row32], gf.at[row32], s_q.at[16 + s], r_q.at[16 + s], at_x(s)))
    for cp in cps:
        cp.wait_recv()
    cp = copy(gf.at[half], gf.at[half], s_q.at[20], r_q.at[20], at_k())
    cp.wait_recv()
    gram_out[...] = gf[...]
    for cp in sends:
        cp.wait_send()


def image_and_gram(matrix, basis):
    dma = pltpu.SemaphoreType.DMA
    nb = BLK - IA
    sems = []
    for shape in (
        (NZ,), (NZ, NY), (NY,), (NZ,),
        (4,), (4,), (4,), (4,),
        (NY,), (NZ,), (NZ,), (NY,), (21,),
    ):
        sems += [dma(shape), dma(shape)]
    return pl.pallas_call(
        kernel,
        out_shape=(
            jax.ShapeDtypeStruct((BLK, KC), F32),
            jax.ShapeDtypeStruct((KC, KC), F32),
        ),
        in_specs=[pl.BlockSpec(memory_space=pl.ANY), pl.BlockSpec(memory_space=pltpu.VMEM)],
        out_specs=(pl.BlockSpec(memory_space=pltpu.VMEM), pl.BlockSpec(memory_space=pltpu.VMEM)),
        scratch_shapes=[
            pltpu.VMEM((8, 2048, 256), BF16),
            pltpu.VMEM((NZ, NY, BLK, KC), BF16),
            pltpu.VMEM((KC, 2048), BF16),
            pltpu.VMEM((4, KC, 256), F32),
            pltpu.VMEM((4, KC, 256), F32),
            pltpu.VMEM((KC, 256), F32),
            pltpu.VMEM((3, KC, 256), F32),
            pltpu.VMEM((3, KC, 256), F32),
            pltpu.VMEM((8, KC, 256), BF16),
            pltpu.VMEM((2048, KC), F32),
            pltpu.VMEM((NY, NZ, IA, KC), IDT),
            pltpu.VMEM((NZ, NY, nb, KC), IDT),
            pltpu.VMEM((NY, NZ, IA, KC), IDT),
            pltpu.VMEM((NZ, NY, nb, KC), IDT),
            pltpu.VMEM((NZ, IA, KC), F32),
            pltpu.VMEM((NY, nb, KC), F32),
            pltpu.VMEM((NZ, IA, KC), F32),
            pltpu.VMEM((NY, nb, KC), F32),
            pltpu.VMEM((KC, KC), F32),
            pltpu.VMEM((128, KC), F32),
            pltpu.VMEM((128, KC), F32),
            pltpu.VMEM((3, 32, KC), F32),
            pltpu.VMEM((32, KC), F32),
            pltpu.VMEM((3, 8, KC), F32),
            pltpu.VMEM((NZ, 8, KC), F32),
            pltpu.VMEM((KC, KC), F32),
            dma((8,)),
            *sems,
        ],
        compiler_params=pltpu.CompilerParams(
            collective_id=0, has_side_effects=True, vmem_limit_bytes=48 * 2**20
        ),
        cost_estimate=pl.CostEstimate(flops=2**33, bytes_accessed=2**23, transcendentals=0),
        name="image_and_gram",
    )(matrix, basis)


def factor(w, n):
    w = list(w)
    ng = len(w)
    row = lax.broadcasted_iota(jnp.int32, (8, n), 0)
    row1 = lax.broadcasted_iota(jnp.int32, (8, 128), 0)
    out = []
    for g in range(ng):
        cur = w[g]
        j0 = 8 * g
        dc = [jnp.broadcast_to(cur[:, j0 + t : j0 + t + 1], (8, 128)) for t in range(8)]
        z = cur
        f = cur
        for t in range(8):
            d = jnp.broadcast_to(dc[t][t : t + 1, :], (8, 128))
            rd = 1.0 / d
            rs = lax.rsqrt(d)
            rdn = jnp.concatenate([rd] * (n // 128), axis=1)
            col = dc[t]
            zrow = jnp.broadcast_to(z[t : t + 1, :], (8, n)) * rdn
            coln = jnp.concatenate([col] * (n // 128), axis=1)
            rsn = jnp.concatenate([rs] * (n // 128), axis=1)
            f = jnp.where(row == t, f * rsn, jnp.where(row > t, z - coln * zrow, f))
            z = jnp.where(row == t, zrow, z - coln * zrow)
            for s in range(t + 1, 8):
                e = jnp.broadcast_to(dc[s][t : t + 1, :], (8, 128)) * rd
                dc[s] = jnp.where(row1 == t, e, dc[s] - col * e)
        out.append(f)
        for i in range(g + 1, ng):
            acc = w[i]
            for t in range(8):
                cc = jnp.broadcast_to(w[i][:, j0 + t : j0 + t + 1], (8, n))
                acc = acc - cc * jnp.broadcast_to(z[t : t + 1, :], (8, n))
            w[i] = acc
    return out

def tail(gram, image, ortho, tri):
    r8 = lax.broadcasted_iota(jnp.int32, (8, 128), 0)
    c8 = lax.broadcasted_iota(jnp.int32, (8, 128), 1)
    eye = [(r8 + 8 * g == c8).astype(F32) for g in range(16)]
    w = [jnp.concatenate([gram[8 * g : 8 * g + 8, :], eye[g]], axis=1) for g in range(16)]
    o = jnp.concatenate(factor(w, 384), axis=0)
    rr = lax.broadcasted_iota(jnp.int32, (128, 128), 0)
    cc = lax.broadcasted_iota(jnp.int32, (128, 128), 1)
    up = cc >= rr
    u11 = jnp.where(up, o[:, :128], 0.0)
    u12 = o[:, 128:256]
    i11 = o[:, 256:]
    a22 = gram[128:, 128:] - lax.dot_general(u12, u12, (((0,), (0,)), ((), ())), precision=lax.Precision.HIGHEST, preferred_element_type=F32)
    q1 = lax.dot_general(image[:, :128], i11, (((1,), (1,)), ((), ())), precision=lax.Precision.HIGHEST, preferred_element_type=F32)
    rest = image[:, 128:] - jnp.dot(q1, u12, precision=lax.Precision.HIGHEST, preferred_element_type=F32)
    w = [jnp.concatenate([a22[8 * g : 8 * g + 8, :], eye[g]], axis=1) for g in range(16)]
    o2 = jnp.concatenate(factor(w, 256), axis=0)
    q2 = lax.dot_general(rest, o2[:, 128:], (((1,), (1,)), ((), ())), precision=lax.Precision.HIGHEST, preferred_element_type=F32)
    ortho[:, :128] = q1
    ortho[:, 128:] = q2
    tri[:128, :128] = u11
    tri[:128, 128:] = u12
    tri[128:, :128] = jnp.zeros((128, 128), F32)
    tri[128:, 128:] = jnp.where(up, o2[:, :128], 0.0)

def orthonormalise(image, gram):
    v = pl.BlockSpec(memory_space=pltpu.VMEM)
    return pl.pallas_call(tail,
        out_shape=(jax.ShapeDtypeStruct(image.shape, F32), jax.ShapeDtypeStruct(gram.shape, F32)),
        in_specs=[v, v], out_specs=(v, v), name="orthonormalise")(gram, image)


def body(matrix, basis):
    return orthonormalise(*image_and_gram(matrix, basis))


def solution(mesh):
    in_specs = (P("row", "col"), P(("row", "col"), None))
    out_specs = (P(("row", "col"), None), P())
    return jax.shard_map(body, mesh=mesh, in_specs=in_specs, out_specs=out_specs, check_vma=False)
```

```python
import jax
import jax.numpy as jnp
from jax import lax
from jax.experimental import pallas as pl
from jax.experimental.pallas import tpu as pltpu
from jax.sharding import PartitionSpec as P

F32 = jnp.float32
BF16 = jnp.bfloat16
NX, NY, NZ = 4, 4, 8
KC = 256
BLK = 64
GA = 48
IA = 48
IDT = BF16
XS = (2, 1, 3, 0)


def kernel(
    a_hbm, basis, img_out, gram_out,
    av, g, bt, part, rk, own, xs, xr, st, im, sa, sb, ya, zb, ta, ub, za, yb,
    g0, gk, g1, gx, gz, gf,
    asem, s_gz, r_gz, s_gzy, r_gzy, s_gy, r_gy, s_gyz, r_gyz,
    s_k, r_k, s_x, r_x, s_sx, r_sx, s_sk, r_sk,
    s_ya, r_ya, s_zb, r_zb, s_za, r_za, s_yb, r_yb,
    s_q, r_q,
):
    r = lax.axis_index("row")
    c = lax.axis_index("col")
    x, k = r // 2, r % 2
    z, y = c // NY, c % NY

    def at_xy(s, t):
        return (((x + s) % NX) * 2 + k, z * NY + (y + t) % NY)

    def at_x(s):
        return at_xy(s, 0)

    def at_k():
        return (x * 2 + 1 - k, c)

    def at_y(s):
        return at_xy(0, s)

    def at_z(s):
        return (r, ((z + s) % NZ) * NY + y)

    shifts = [(s, t) for s in range(NX) for t in range(NY) if s or t]
    far = (4, 3, 5, 2, 6, 1, 7)
    near = (1, 7, 2, 6, 3, 5, 4)
    halves = range(2)

    loads = []
    for j in range(8):
        cp = pltpu.make_async_copy(a_hbm.at[:, pl.ds(256 * j, 256)], av.at[j], asem.at[j])
        cp.start()
        loads.append(cp)

    barrier = pltpu.get_barrier_semaphore()
    for s in far:
        pl.semaphore_signal(barrier, 1, device_id=at_z(s))
    for s, t in shifts:
        pl.semaphore_signal(barrier, 1, device_id=at_xy(s, t))
    pl.semaphore_signal(barrier, 1, device_id=at_k())
    for h in halves:
        g[h, z, y] = basis[:, 128 * h : 128 * h + 128]
    pl.semaphore_wait(barrier, NZ - 1 + NX * NY - 1 + 1)

    sends = []

    def copy(src, dst, ss, rs, dev):
        cp = pltpu.make_async_remote_copy(src, dst, ss, rs, device_id=dev)
        cp.start()
        sends.append(cp)
        return cp

    hi, lo = pl.ds(0, GA), pl.ds(GA, BLK - GA)
    cy, cz, cyz, czy = {}, {}, {}, {}
    for h in halves:
        k128 = pl.ds(128 * h, 128)
        for s in near:
            cz[h, s] = copy(basis.at[hi, k128], g.at[h, z, y, hi], s_gz.at[h, s], r_gz.at[h, s], at_z(s))
        for s in (2, 1, 3):
            cy[h, s] = copy(basis.at[lo, k128], g.at[h, z, y, lo], s_gy.at[h, s], r_gy.at[h, s], at_y(s))
        for t in (2, 1, 3):
            czy[h, 0, t] = copy(basis.at[hi, k128], g.at[h, z, y, hi], s_gzy.at[h, 0, t], r_gzy.at[h, 0, t], at_y(t))
    for h in halves:
        for s in (1, 3, 2):
            cy[h, s].wait_recv()
        for s in far:
            cyz[h, s] = copy(g.at[h, z, :, lo], g.at[h, z, :, lo], s_gyz.at[h, s], r_gyz.at[h, s], at_z(s))
        for s in near:
            cz[h, s].wait_recv()
            zs = (z + NZ - s) % NZ
            for t in (2, 1, 3):
                czy[h, s, t] = copy(
                    g.at[h, zs, y, hi], g.at[h, zs, y, hi], s_gzy.at[h, s, t], r_gzy.at[h, s, t], at_y(t)
                )

    def product(h, j):
        return jnp.dot(bt[h], av[j], preferred_element_type=F32)

    cx = {}
    for h in halves:
        for s in far:
            cyz[h, s].wait_recv()
        for s in (0, *near):
            for t in (1, 3, 2):
                czy[h, s, t].wait_recv()

        def turn(i, carry):
            bt[h, :, pl.ds(pl.multiple_of(i * 256, 256), 256)] = g[h, i].reshape(NY * BLK, 128).T
            return carry

        lax.fori_loop(0, NZ, turn, 0)
        if h == 0:
            for cp in loads:
                cp.wait()
        ck = []
        for i, s in enumerate(XS):
            part[h, i] = product(h, 2 * ((x + s) % NX) + 1 - k)
            ck.append(copy(part.at[h, i], rk.at[h, i], s_k.at[h, i], r_k.at[h, i], at_k()))
        for i, s in enumerate(XS):
            p = product(h, 2 * ((x + s) % NX) + k)
            ck[i].wait_recv()
            p = p + rk[h, i]
            if s:
                xs[h, i] = p
                cx[h, i] = copy(xs.at[h, i], xr.at[h, i], s_x.at[h, i], r_x.at[h, i], at_x(s))
            else:
                own[h] = p
    csx, csk = {}, {}
    for h in halves:
        for i in (1, 2, 0):
            cx[h, i].wait_recv()
        total = (own[h] + xr[h, 0]) + (xr[h, 1] + xr[h, 2])
        st[h, r] = (total * (16384.0**-0.5)).astype(BF16)
        mine = st.at[h, r]
        for s in (2, 1, 3):
            csx[h, s] = copy(mine, mine, s_sx.at[h, s], r_sx.at[h, s], at_x(s))
        csk[h, 0] = copy(mine, mine, s_sk.at[h, 0], r_sk.at[h, 0], at_k())

    nb = BLK - IA
    cya, czb, cza, cyb = {}, {}, {}, {}
    for h in halves:

        def add(ja, jb, first):
            def tile(i, carry):
                rows = pl.ds(pl.multiple_of(i * 256, 256), 256)
                dims = (((1,), (1,)), ((), ()))
                v = lax.dot_general(av[ja, rows, :], st[h, ja], dims, preferred_element_type=F32)
                v += lax.dot_general(av[jb, rows, :], st[h, jb], dims, preferred_element_type=F32)
                if not first:
                    v += im[h, rows, :]
                im[h, rows, :] = v
                return carry

            lax.fori_loop(0, 8, tile, 0)

        csk[h, 0].wait_recv()
        add(r, x * 2 + 1 - k, True)
        for s in (1, 3, 2):
            csx[h, s].wait_recv()
            j = 2 * ((x + NX - s) % NX) + k
            csk[h, s] = copy(st.at[h, j], st.at[h, j], s_sk.at[h, s], r_sk.at[h, s], at_k())
        for s in (1, 3, 2):
            csk[h, s].wait_recv()
            xq = (x + NX - s) % NX
            add(2 * xq + k, 2 * xq + 1 - k, False)
        v4 = im.reshape(2, NZ, NY, BLK, 128)
        for s in (2, 1, 3):
            sa[h, s] = v4[h, :, (y + s) % NY, :IA, :].astype(IDT)
            cya[h, s] = copy(sa.at[h, s], ya.at[h, s], s_ya.at[h, s], r_ya.at[h, s], at_y(s))
        for s in far:
            sb[h, s] = v4[h, (z + s) % NZ, :, IA:, :].astype(IDT)
            czb[h, s] = copy(sb.at[h, s], zb.at[h, s], s_zb.at[h, s], r_zb.at[h, s], at_z(s))
        ta[h] = v4[h, :, y, :IA, :]
        ub[h] = v4[h, z, :, IA:, :]
    for h in halves:
        for s in (1, 3, 2):
            cya[h, s].wait_recv()
        ta[h] = (ta[h] + ya[h, 1].astype(F32)) + (ya[h, 2].astype(F32) + ya[h, 3].astype(F32))
        for s in far:
            cza[h, s] = copy(ta.at[h, (z + s) % NZ], za.at[h, s], s_za.at[h, s], r_za.at[h, s], at_z(s))
        u = ub[h]
        for s in near:
            czb[h, s].wait_recv()
            u = u + zb[h, s].astype(F32)
        ub[h] = u
        for s in (2, 1, 3):
            cyb[h, s] = copy(ub.at[h, (y + s) % NY], yb.at[h, s], s_yb.at[h, s], r_yb.at[h, s], at_y(s))
    scale = 65536.0**-0.5
    for h in halves:
        low = ub[h, y]
        for s in (1, 3, 2):
            cyb[h, s].wait_recv()
            low = low + yb[h, s]
        high = ta[h, z]
        for s in near:
            cza[h, s].wait_recv()
            high = high + za[h, s]
        img_out[:IA, 128 * h : 128 * h + 128] = high * scale
        img_out[IA:, 128 * h : 128 * h + 128] = low * scale

    img = img_out[...]
    g0[...] = lax.dot_general(
        img, img, (((0,), (0,)), ((), ())),
        precision=lax.Precision.HIGHEST, preferred_element_type=F32,
    ) * (1.0 / 16384.0)
    half = pl.multiple_of(128 * k, 128)
    cp = copy(g0.at[pl.ds(pl.multiple_of(128 * (1 - k), 128), 128)], gk, s_q.at[0], r_q.at[0], at_k())
    cp.wait_recv()
    g1[...] = g0[pl.ds(half, 128), :] + gk[...]

    def rows8(xq, yq):
        return pl.ds(pl.multiple_of(32 * xq + 8 * yq, 8), 8)

    cps = []
    for s, t in sorted(shifts, key=lambda v: -min(v[0], NX - v[0]) - min(v[1], NY - v[1])):
        q = NY * s + t
        piece = g1.at[rows8((x + s) % NX, (y + t) % NY)]
        cps.append(copy(piece, gx.at[q], s_q.at[q], r_q.at[q], at_xy(s, t)))
    acc = g1[rows8(x, y), :]
    for (s, t), cp in zip(reversed(shifts), reversed(cps)):
        cp.wait_recv()
    for s, t in shifts:
        acc = acc + gx[NY * s + t]
    gz[z] = acc
    cps = []
    for s in far:
        cps.append(copy(gz.at[z], gz.at[z], s_q.at[15 + s], r_q.at[15 + s], at_z(s)))
    for cp in cps:
        cp.wait_recv()
    row8 = pl.ds(pl.multiple_of(half + 32 * x + 8 * y, 8), 8)
    gf[row8, :] = ((gz[0] + gz[1]) + (gz[2] + gz[3])) + ((gz[4] + gz[5]) + (gz[6] + gz[7]))
    cps = {}
    for s, t in sorted(shifts, key=lambda v: -min(v[0], NX - v[0]) - min(v[1], NY - v[1])):
        q = 23 + NY * s + t
        cps[s, t] = copy(gf.at[row8], gf.at[row8], s_q.at[q], r_q.at[q], at_xy(s, t))
    ckf = []
    for s in (0, 1, 3, 2):
        for t in range(NY):
            if s or t:
                cps[s, t].wait_recv()
        row32 = gf.at[pl.ds(pl.multiple_of(half + 32 * ((x + NX - s) % NX), 32), 32)]
        ckf.append(copy(row32, row32, s_q.at[39 + s], r_q.at[39 + s], at_k()))
    for cp in ckf:
        cp.wait_recv()
    gram_out[...] = gf[...]
    for cp in sends:
        cp.wait_send()


def image_and_gram(matrix, basis):
    dma = pltpu.SemaphoreType.DMA
    nb = BLK - IA
    sems = []
    for shape in (
        (2, NZ), (2, NZ, NY), (2, NY), (2, NZ),
        (2, 4), (2, 3), (2, 4), (2, 4),
        (2, NY), (2, NZ), (2, NZ), (2, NY), (43,),
    ):
        sems += [dma(shape), dma(shape)]
    return pl.pallas_call(
        kernel,
        out_shape=(
            jax.ShapeDtypeStruct((BLK, KC), F32),
            jax.ShapeDtypeStruct((KC, KC), F32),
        ),
        in_specs=[pl.BlockSpec(memory_space=pl.ANY), pl.BlockSpec(memory_space=pltpu.VMEM)],
        out_specs=(pl.BlockSpec(memory_space=pltpu.VMEM), pl.BlockSpec(memory_space=pltpu.VMEM)),
        scratch_shapes=[
            pltpu.VMEM((8, 2048, 256), BF16),
            pltpu.VMEM((2, NZ, NY, BLK, 128), BF16),
            pltpu.VMEM((2, 128, 2048), BF16),
            pltpu.VMEM((2, 4, 128, 256), F32),
            pltpu.VMEM((2, 4, 128, 256), F32),
            pltpu.VMEM((2, 128, 256), F32),
            pltpu.VMEM((2, 3, 128, 256), F32),
            pltpu.VMEM((2, 3, 128, 256), F32),
            pltpu.VMEM((2, 8, 128, 256), BF16),
            pltpu.VMEM((2, 2048, 128), F32),
            pltpu.VMEM((2, NY, NZ, IA, 128), IDT),
            pltpu.VMEM((2, NZ, NY, nb, 128), IDT),
            pltpu.VMEM((2, NY, NZ, IA, 128), IDT),
            pltpu.VMEM((2, NZ, NY, nb, 128), IDT),
            pltpu.VMEM((2, NZ, IA, 128), F32),
            pltpu.VMEM((2, NY, nb, 128), F32),
            pltpu.VMEM((2, NZ, IA, 128), F32),
            pltpu.VMEM((2, NY, nb, 128), F32),
            pltpu.VMEM((KC, KC), F32),
            pltpu.VMEM((128, KC), F32),
            pltpu.VMEM((128, KC), F32),
            pltpu.VMEM((NX * NY, 8, KC), F32),
            pltpu.VMEM((NZ, 8, KC), F32),
            pltpu.VMEM((KC, KC), F32),
            dma((8,)),
            *sems,
        ],
        compiler_params=pltpu.CompilerParams(
            collective_id=0, has_side_effects=True, vmem_limit_bytes=48 * 2**20
        ),
        cost_estimate=pl.CostEstimate(flops=2**33, bytes_accessed=2**23, transcendentals=0),
        name="image_and_gram",
    )(matrix, basis)


def factor(w, n):
    w = list(w)
    ng = len(w)
    row = lax.broadcasted_iota(jnp.int32, (8, n), 0)
    row1 = lax.broadcasted_iota(jnp.int32, (8, 128), 0)
    out = []
    for g in range(ng):
        cur = w[g]
        j0 = 8 * g
        dc = [jnp.broadcast_to(cur[:, j0 + t : j0 + t + 1], (8, 128)) for t in range(8)]
        z = cur
        f = cur
        for t in range(8):
            d = jnp.broadcast_to(dc[t][t : t + 1, :], (8, 128))
            rd = 1.0 / d
            rs = lax.rsqrt(d)
            rdn = jnp.concatenate([rd] * (n // 128), axis=1)
            col = dc[t]
            zrow = jnp.broadcast_to(z[t : t + 1, :], (8, n)) * rdn
            coln = jnp.concatenate([col] * (n // 128), axis=1)
            rsn = jnp.concatenate([rs] * (n // 128), axis=1)
            f = jnp.where(row == t, f * rsn, jnp.where(row > t, z - coln * zrow, f))
            z = jnp.where(row == t, zrow, z - coln * zrow)
            for s in range(t + 1, 8):
                e = jnp.broadcast_to(dc[s][t : t + 1, :], (8, 128)) * rd
                dc[s] = jnp.where(row1 == t, e, dc[s] - col * e)
        out.append(f)
        for i in range(g + 1, ng):
            acc = w[i]
            for t in range(8):
                cc = jnp.broadcast_to(w[i][:, j0 + t : j0 + t + 1], (8, n))
                acc = acc - cc * jnp.broadcast_to(z[t : t + 1, :], (8, n))
            w[i] = acc
    return out

def tail(gram, image, ortho, tri):
    r8 = lax.broadcasted_iota(jnp.int32, (8, 128), 0)
    c8 = lax.broadcasted_iota(jnp.int32, (8, 128), 1)
    eye = [(r8 + 8 * g == c8).astype(F32) for g in range(16)]
    w = [jnp.concatenate([gram[8 * g : 8 * g + 8, :], eye[g]], axis=1) for g in range(16)]
    o = jnp.concatenate(factor(w, 384), axis=0)
    rr = lax.broadcasted_iota(jnp.int32, (128, 128), 0)
    cc = lax.broadcasted_iota(jnp.int32, (128, 128), 1)
    up = cc >= rr
    u11 = jnp.where(up, o[:, :128], 0.0)
    u12 = o[:, 128:256]
    i11 = o[:, 256:]
    a22 = gram[128:, 128:] - lax.dot_general(u12, u12, (((0,), (0,)), ((), ())), precision=lax.Precision.HIGHEST, preferred_element_type=F32)
    q1 = lax.dot_general(image[:, :128], i11, (((1,), (1,)), ((), ())), precision=lax.Precision.HIGHEST, preferred_element_type=F32)
    rest = image[:, 128:] - jnp.dot(q1, u12, precision=lax.Precision.HIGHEST, preferred_element_type=F32)
    w = [jnp.concatenate([a22[8 * g : 8 * g + 8, :], eye[g]], axis=1) for g in range(16)]
    o2 = jnp.concatenate(factor(w, 256), axis=0)
    q2 = lax.dot_general(rest, o2[:, 128:], (((1,), (1,)), ((), ())), precision=lax.Precision.HIGHEST, preferred_element_type=F32)
    ortho[:, :128] = q1
    ortho[:, 128:] = q2
    tri[:128, :128] = u11
    tri[:128, 128:] = u12
    tri[128:, :128] = jnp.zeros((128, 128), F32)
    tri[128:, 128:] = jnp.where(up, o2[:, :128], 0.0)

def orthonormalise(image, gram):
    v = pl.BlockSpec(memory_space=pltpu.VMEM)
    return pl.pallas_call(tail,
        out_shape=(jax.ShapeDtypeStruct(image.shape, F32), jax.ShapeDtypeStruct(gram.shape, F32)),
        in_specs=[v, v], out_specs=(v, v), name="orthonormalise")(gram, image)


def body(matrix, basis):
    return orthonormalise(*image_and_gram(matrix, basis))


def solution(mesh):
    in_specs = (P("row", "col"), P(("row", "col"), None))
    out_specs = (P(("row", "col"), None), P())
    return jax.shard_map(body, mesh=mesh, in_specs=in_specs, out_specs=out_specs, check_vma=False)
```

```python
import jax
import jax.numpy as jnp
from jax import lax
from jax.experimental import pallas as pl
from jax.experimental.pallas import tpu as pltpu
from jax.sharding import PartitionSpec as P

F32 = jnp.float32
BF16 = jnp.bfloat16
NX, NY, NZ = 4, 4, 8
KC = 256
BLK = 64
GA = 48
IA = 48
IDT = BF16
XS = (2, 1, 3, 0)


def kernel(
    a_hbm, b_hbm, img_out, gram_out,
    av, basis, g, bt, part, rk, own, xs, xr, st, im, sa, sb, ya, zb, ta, ub, za, yb,
    g0, gk, g1, gx, gz, gf,
    asem, s_gz, r_gz, s_gzy, r_gzy, s_gy, r_gy, s_gyz, r_gyz,
    s_k, r_k, s_x, r_x, s_sx, r_sx, s_sk, r_sk,
    s_ya, r_ya, s_zb, r_zb, s_za, r_za, s_yb, r_yb,
    s_q, r_q,
):
    r = lax.axis_index("row")
    c = lax.axis_index("col")
    x, k = r // 2, r % 2
    z, y = c // NY, c % NY

    def at_xy(s, t):
        return (((x + s) % NX) * 2 + k, z * NY + (y + t) % NY)

    def at_x(s):
        return at_xy(s, 0)

    def at_k():
        return (x * 2 + 1 - k, c)

    def at_y(s):
        return at_xy(0, s)

    def at_z(s):
        return (r, ((z + s) % NZ) * NY + y)

    shifts = [(s, t) for s in range(NX) for t in range(NY) if s or t]
    far = (4, 3, 5, 2, 6, 1, 7)
    near = (1, 7, 2, 6, 3, 5, 4)
    halves = range(2)

    first = pltpu.make_async_copy(b_hbm, basis, asem.at[8])
    first.start()
    loads = []
    for j in range(8):
        cp = pltpu.make_async_copy(a_hbm.at[:, pl.ds(256 * j, 256)], av.at[j], asem.at[j])
        cp.start()
        loads.append(cp)

    barrier = pltpu.get_barrier_semaphore()
    for s in far:
        pl.semaphore_signal(barrier, 1, device_id=at_z(s))
    for s in range(1, NY):
        pl.semaphore_signal(barrier, 1, device_id=at_y(s))
    for s in range(1, NX):
        pl.semaphore_signal(barrier, 1, device_id=at_x(s))
    pl.semaphore_signal(barrier, 1, device_id=at_k())
    first.wait()
    for h in halves:
        g[h, z, y] = basis[:, 128 * h : 128 * h + 128]
    pl.semaphore_wait(barrier, NZ + NY + NX - 3 + 1)

    sends = []

    def copy(src, dst, ss, rs, dev):
        cp = pltpu.make_async_remote_copy(src, dst, ss, rs, device_id=dev)
        cp.start()
        sends.append(cp)
        return cp

    hi, lo = pl.ds(0, GA), pl.ds(GA, BLK - GA)
    cy, cz, cyz, czy = {}, {}, {}, {}
    for h in halves:
        k128 = pl.ds(128 * h, 128)
        for s in near:
            cz[h, s] = copy(basis.at[hi, k128], g.at[h, z, y, hi], s_gz.at[h, s], r_gz.at[h, s], at_z(s))
        for s in (2, 1, 3):
            cy[h, s] = copy(basis.at[lo, k128], g.at[h, z, y, lo], s_gy.at[h, s], r_gy.at[h, s], at_y(s))
        for t in (2, 1, 3):
            czy[h, 0, t] = copy(basis.at[hi, k128], g.at[h, z, y, hi], s_gzy.at[h, 0, t], r_gzy.at[h, 0, t], at_y(t))
    for h in halves:
        for s in (1, 3, 2):
            cy[h, s].wait_recv()
        for s in far:
            cyz[h, s] = copy(g.at[h, z, :, lo], g.at[h, z, :, lo], s_gyz.at[h, s], r_gyz.at[h, s], at_z(s))
        for s in near:
            cz[h, s].wait_recv()
            zs = (z + NZ - s) % NZ
            for t in (2, 1, 3):
                czy[h, s, t] = copy(
                    g.at[h, zs, y, hi], g.at[h, zs, y, hi], s_gzy.at[h, s, t], r_gzy.at[h, s, t], at_y(t)
                )

    def product(h, j):
        return jnp.dot(bt[h], av[j], preferred_element_type=F32)

    cx = {}
    for h in halves:
        for s in far:
            cyz[h, s].wait_recv()
        for s in (0, *near):
            for t in (1, 3, 2):
                czy[h, s, t].wait_recv()

        for i in range(NZ):
            bt[h, :, 256 * i : 256 * i + 256] = g[h, i].reshape(NY * BLK, 128).T
        if h == 0:
            for cp in loads:
                cp.wait()
        ck = []
        for i, s in enumerate(XS):
            part[h, i] = product(h, 2 * ((x + s) % NX) + 1 - k)
            ck.append(copy(part.at[h, i], rk.at[h, i], s_k.at[h, i], r_k.at[h, i], at_k()))
        for i, s in enumerate(XS):
            p = product(h, 2 * ((x + s) % NX) + k)
            ck[i].wait_recv()
            p = p + rk[h, i]
            if s:
                xs[h, i] = p
                cx[h, i] = copy(xs.at[h, i], xr.at[h, i], s_x.at[h, i], r_x.at[h, i], at_x(s))
            else:
                own[h] = p
    csx, csk = {}, {}
    for h in halves:
        for i in (1, 2, 0):
            cx[h, i].wait_recv()
        total = (own[h] + xr[h, 0]) + (xr[h, 1] + xr[h, 2])
        st[h, r] = (total * (16384.0**-0.5)).astype(BF16)
        mine = st.at[h, r]
        for s in (2, 1, 3):
            csx[h, s] = copy(mine, mine, s_sx.at[h, s], r_sx.at[h, s], at_x(s))
        csk[h, 0] = copy(mine, mine, s_sk.at[h, 0], r_sk.at[h, 0], at_k())

    nb = BLK - IA
    cya, czb, cza, cyb = {}, {}, {}, {}
    for h in halves:

        def add(ja, jb, first):
            dims = (((1,), (1,)), ((), ()))
            for i in range(8):
                rows = pl.ds(256 * i, 256)
                v = lax.dot_general(av[ja, rows, :], st[h, ja], dims, preferred_element_type=F32)
                v += lax.dot_general(av[jb, rows, :], st[h, jb], dims, preferred_element_type=F32)
                if not first:
                    v += im[h, rows, :]
                im[h, rows, :] = v

        csk[h, 0].wait_recv()
        add(r, x * 2 + 1 - k, True)
        for s in (1, 3, 2):
            csx[h, s].wait_recv()
            j = 2 * ((x + NX - s) % NX) + k
            csk[h, s] = copy(st.at[h, j], st.at[h, j], s_sk.at[h, s], r_sk.at[h, s], at_k())
        for s in (1, 3, 2):
            csk[h, s].wait_recv()
            xq = (x + NX - s) % NX
            add(2 * xq + k, 2 * xq + 1 - k, False)
        v4 = im.reshape(2, NZ, NY, BLK, 128)
        for s in (2, 1, 3):
            sa[h, s] = v4[h, :, (y + s) % NY, :IA, :].astype(IDT)
            cya[h, s] = copy(sa.at[h, s], ya.at[h, s], s_ya.at[h, s], r_ya.at[h, s], at_y(s))
        for s in far:
            sb[h, s] = v4[h, (z + s) % NZ, :, IA:, :].astype(IDT)
            czb[h, s] = copy(sb.at[h, s], zb.at[h, s], s_zb.at[h, s], r_zb.at[h, s], at_z(s))
        ta[h] = v4[h, :, y, :IA, :]
        ub[h] = v4[h, z, :, IA:, :]
    for h in halves:
        for s in (1, 3, 2):
            cya[h, s].wait_recv()
        ta[h] = (ta[h] + ya[h, 1].astype(F32)) + (ya[h, 2].astype(F32) + ya[h, 3].astype(F32))
        for s in far:
            cza[h, s] = copy(ta.at[h, (z + s) % NZ], za.at[h, s], s_za.at[h, s], r_za.at[h, s], at_z(s))
        u = ub[h]
        for s in near:
            czb[h, s].wait_recv()
            u = u + zb[h, s].astype(F32)
        ub[h] = u
        for s in (2, 1, 3):
            cyb[h, s] = copy(ub.at[h, (y + s) % NY], yb.at[h, s], s_yb.at[h, s], r_yb.at[h, s], at_y(s))
    scale = 65536.0**-0.5
    for h in halves:
        low = ub[h, y]
        for s in (1, 3, 2):
            cyb[h, s].wait_recv()
            low = low + yb[h, s]
        high = ta[h, z]
        for s in near:
            cza[h, s].wait_recv()
            high = high + za[h, s]
        img_out[:IA, 128 * h : 128 * h + 128] = high * scale
        img_out[IA:, 128 * h : 128 * h + 128] = low * scale

    img = img_out[...]
    g0[...] = lax.dot_general(
        img, img, (((0,), (0,)), ((), ())),
        precision=lax.Precision.HIGHEST, preferred_element_type=F32,
    ) * (1.0 / 16384.0)
    half = pl.multiple_of(128 * k, 128)
    cp = copy(g0.at[pl.ds(pl.multiple_of(128 * (1 - k), 128), 128)], gk, s_q.at[0], r_q.at[0], at_k())
    cp.wait_recv()
    g1[...] = g0[pl.ds(half, 128), :] + gk[...]

    def rows8(xq, yq):
        return pl.ds(pl.multiple_of(32 * xq + 8 * yq, 8), 8)

    cps = []
    for s, t in sorted(shifts, key=lambda v: -min(v[0], NX - v[0]) - min(v[1], NY - v[1])):
        q = NY * s + t
        piece = g1.at[rows8((x + s) % NX, (y + t) % NY)]
        cps.append(copy(piece, gx.at[q], s_q.at[q], r_q.at[q], at_xy(s, t)))
    acc = g1[rows8(x, y), :]
    for (s, t), cp in zip(reversed(shifts), reversed(cps)):
        cp.wait_recv()
    for s, t in shifts:
        acc = acc + gx[NY * s + t]
    gz[z] = acc
    cps = []
    for s in far:
        cps.append(copy(gz.at[z], gz.at[z], s_q.at[15 + s], r_q.at[15 + s], at_z(s)))
    for cp in cps:
        cp.wait_recv()
    row8 = pl.ds(pl.multiple_of(half + 32 * x + 8 * y, 8), 8)
    gf[row8, :] = ((gz[0] + gz[1]) + (gz[2] + gz[3])) + ((gz[4] + gz[5]) + (gz[6] + gz[7]))
    cps = {}
    for s, t in sorted(shifts, key=lambda v: -min(v[0], NX - v[0]) - min(v[1], NY - v[1])):
        q = 23 + NY * s + t
        cps[s, t] = copy(gf.at[row8], gf.at[row8], s_q.at[q], r_q.at[q], at_xy(s, t))
    ckf = []
    for s in (0, 1, 3, 2):
        for t in range(NY):
            if s or t:
                cps[s, t].wait_recv()
        row32 = gf.at[pl.ds(pl.multiple_of(half + 32 * ((x + NX - s) % NX), 32), 32)]
        ckf.append(copy(row32, row32, s_q.at[39 + s], r_q.at[39 + s], at_k()))
    for cp in ckf:
        cp.wait_recv()
    gram_out[...] = gf[...]
    for cp in sends:
        cp.wait_send()


def image_and_gram(matrix, basis):
    dma = pltpu.SemaphoreType.DMA
    nb = BLK - IA
    sems = []
    for shape in (
        (2, NZ), (2, NZ, NY), (2, NY), (2, NZ),
        (2, 4), (2, 3), (2, 4), (2, 4),
        (2, NY), (2, NZ), (2, NZ), (2, NY), (43,),
    ):
        sems += [dma(shape), dma(shape)]
    return pl.pallas_call(
        kernel,
        out_shape=(
            jax.ShapeDtypeStruct((BLK, KC), F32),
            jax.ShapeDtypeStruct((KC, KC), F32),
        ),
        in_specs=[pl.BlockSpec(memory_space=pltpu.HBM)] * 2,
        out_specs=(pl.BlockSpec(memory_space=pltpu.VMEM), pl.BlockSpec(memory_space=pltpu.VMEM)),
        scratch_shapes=[
            pltpu.VMEM((8, 2048, 256), BF16),
            pltpu.VMEM((BLK, KC), BF16),
            pltpu.VMEM((2, NZ, NY, BLK, 128), BF16),
            pltpu.VMEM((2, 128, 2048), BF16),
            pltpu.VMEM((2, 4, 128, 256), F32),
            pltpu.VMEM((2, 4, 128, 256), F32),
            pltpu.VMEM((2, 128, 256), F32),
            pltpu.VMEM((2, 3, 128, 256), F32),
            pltpu.VMEM((2, 3, 128, 256), F32),
            pltpu.VMEM((2, 8, 128, 256), BF16),
            pltpu.VMEM((2, 2048, 128), F32),
            pltpu.VMEM((2, NY, NZ, IA, 128), IDT),
            pltpu.VMEM((2, NZ, NY, nb, 128), IDT),
            pltpu.VMEM((2, NY, NZ, IA, 128), IDT),
            pltpu.VMEM((2, NZ, NY, nb, 128), IDT),
            pltpu.VMEM((2, NZ, IA, 128), F32),
            pltpu.VMEM((2, NY, nb, 128), F32),
            pltpu.VMEM((2, NZ, IA, 128), F32),
            pltpu.VMEM((2, NY, nb, 128), F32),
            pltpu.VMEM((KC, KC), F32),
            pltpu.VMEM((128, KC), F32),
            pltpu.VMEM((128, KC), F32),
            pltpu.VMEM((NX * NY, 8, KC), F32),
            pltpu.VMEM((NZ, 8, KC), F32),
            pltpu.VMEM((KC, KC), F32),
            dma((9,)),
            *sems,
        ],
        compiler_params=pltpu.CompilerParams(
            collective_id=0, has_side_effects=True, vmem_limit_bytes=48 * 2**20
        ),
        cost_estimate=pl.CostEstimate(flops=2**33, bytes_accessed=2**23, transcendentals=0),
        name="image_and_gram",
    )(matrix, basis)


def factor(w, n):
    w = list(w)
    ng = len(w)
    row = lax.broadcasted_iota(jnp.int32, (8, n), 0)
    row1 = lax.broadcasted_iota(jnp.int32, (8, 128), 0)
    out = []
    for g in range(ng):
        cur = w[g]
        j0 = 8 * g
        dc = [jnp.broadcast_to(cur[:, j0 + t : j0 + t + 1], (8, 128)) for t in range(8)]
        z = cur
        f = cur
        for t in range(8):
            d = jnp.broadcast_to(dc[t][t : t + 1, :], (8, 128))
            rd = 1.0 / d
            rs = lax.rsqrt(d)
            rdn = jnp.concatenate([rd] * (n // 128), axis=1)
            col = dc[t]
            zrow = jnp.broadcast_to(z[t : t + 1, :], (8, n)) * rdn
            coln = jnp.concatenate([col] * (n // 128), axis=1)
            rsn = jnp.concatenate([rs] * (n // 128), axis=1)
            f = jnp.where(row == t, f * rsn, jnp.where(row > t, z - coln * zrow, f))
            z = jnp.where(row == t, zrow, z - coln * zrow)
            for s in range(t + 1, 8):
                e = jnp.broadcast_to(dc[s][t : t + 1, :], (8, 128)) * rd
                dc[s] = jnp.where(row1 == t, e, dc[s] - col * e)
        out.append(f)
        for i in range(g + 1, ng):
            acc = w[i]
            for t in range(8):
                cc = jnp.broadcast_to(w[i][:, j0 + t : j0 + t + 1], (8, n))
                acc = acc - cc * jnp.broadcast_to(z[t : t + 1, :], (8, n))
            w[i] = acc
    return out

def tail(gram, image, ortho, tri):
    r8 = lax.broadcasted_iota(jnp.int32, (8, 128), 0)
    c8 = lax.broadcasted_iota(jnp.int32, (8, 128), 1)
    eye = [(r8 + 8 * g == c8).astype(F32) for g in range(16)]
    w = [jnp.concatenate([gram[8 * g : 8 * g + 8, :], eye[g]], axis=1) for g in range(16)]
    o = jnp.concatenate(factor(w, 384), axis=0)
    rr = lax.broadcasted_iota(jnp.int32, (128, 128), 0)
    cc = lax.broadcasted_iota(jnp.int32, (128, 128), 1)
    up = cc >= rr
    u11 = jnp.where(up, o[:, :128], 0.0)
    u12 = o[:, 128:256]
    i11 = o[:, 256:]
    a22 = gram[128:, 128:] - lax.dot_general(u12, u12, (((0,), (0,)), ((), ())), precision=lax.Precision.HIGHEST, preferred_element_type=F32)
    q1 = lax.dot_general(image[:, :128], i11, (((1,), (1,)), ((), ())), precision=lax.Precision.HIGHEST, preferred_element_type=F32)
    rest = image[:, 128:] - jnp.dot(q1, u12, precision=lax.Precision.HIGHEST, preferred_element_type=F32)
    w = [jnp.concatenate([a22[8 * g : 8 * g + 8, :], eye[g]], axis=1) for g in range(16)]
    o2 = jnp.concatenate(factor(w, 256), axis=0)
    q2 = lax.dot_general(rest, o2[:, 128:], (((1,), (1,)), ((), ())), precision=lax.Precision.HIGHEST, preferred_element_type=F32)
    ortho[:, :128] = q1
    ortho[:, 128:] = q2
    tri[:128, :128] = u11
    tri[:128, 128:] = u12
    tri[128:, :128] = jnp.zeros((128, 128), F32)
    tri[128:, 128:] = jnp.where(up, o2[:, :128], 0.0)

def orthonormalise(image, gram):
    v = pl.BlockSpec(memory_space=pltpu.VMEM)
    return pl.pallas_call(tail,
        out_shape=(jax.ShapeDtypeStruct(image.shape, F32), jax.ShapeDtypeStruct(gram.shape, F32)),
        in_specs=[v, v], out_specs=(v, v), name="orthonormalise",
        compiler_params=pltpu.CompilerParams(vmem_limit_bytes=16 * 2**20))(gram, image)


def body(matrix, basis):
    return orthonormalise(*image_and_gram(matrix, basis))


def solution(mesh):
    in_specs = (P("row", "col"), P(("row", "col"), None))
    out_specs = (P(("row", "col"), None), P())
    return jax.shard_map(body, mesh=mesh, in_specs=in_specs, out_specs=out_specs, check_vma=False)
```

```python
import jax
import jax.numpy as jnp
from jax import lax
from jax.experimental import pallas as pl
from jax.experimental.pallas import tpu as pltpu
from jax.sharding import PartitionSpec as P

F32 = jnp.float32
BF16 = jnp.bfloat16
NX, NY, NZ = 4, 4, 8
KC = 256
BLK = 64
GA = 48
IA = 48
IDT = BF16
XS = (2, 1, 3, 0)
XFAR, XNEAR = BF16, F32


def kernel(
    a_hbm, b_hbm, img_out, gram_out,
    av, basis, g, bt, part, rk, own, xs2, xs1, xr2, xr1, st, im, sa, sb, ya, zb, ta, ub, za, yb,
    g0, gk, g1, gx, gz, gf,
    asem, s_gz, r_gz, s_gzy, r_gzy, s_gy, r_gy, s_gyz, r_gyz,
    s_k, r_k, s_x, r_x, s_sx, r_sx, s_sk, r_sk,
    s_ya, r_ya, s_zb, r_zb, s_za, r_za, s_yb, r_yb,
    s_q, r_q,
):
    r = lax.axis_index("row")
    c = lax.axis_index("col")
    x, k = r // 2, r % 2
    z, y = c // NY, c % NY

    def at_xy(s, t):
        return (((x + s) % NX) * 2 + k, z * NY + (y + t) % NY)

    def at_x(s):
        return at_xy(s, 0)

    def at_k():
        return (x * 2 + 1 - k, c)

    def at_y(s):
        return at_xy(0, s)

    def at_z(s):
        return (r, ((z + s) % NZ) * NY + y)

    shifts = [(s, t) for s in range(NX) for t in range(NY) if s or t]
    far = (4, 3, 5, 2, 6, 1, 7)
    near = (1, 7, 2, 6, 3, 5, 4)
    halves = range(2)

    first = pltpu.make_async_copy(b_hbm, basis, asem.at[8])
    first.start()
    loads = []
    for j in range(8):
        cp = pltpu.make_async_copy(a_hbm.at[:, pl.ds(256 * j, 256)], av.at[j], asem.at[j])
        cp.start()
        loads.append(cp)

    barrier = pltpu.get_barrier_semaphore()
    for s in far:
        pl.semaphore_signal(barrier, 1, device_id=at_z(s))
    for s in range(1, NY):
        pl.semaphore_signal(barrier, 1, device_id=at_y(s))
    for s in range(1, NX):
        pl.semaphore_signal(barrier, 1, device_id=at_x(s))
    pl.semaphore_signal(barrier, 1, device_id=at_k())
    first.wait()
    for h in halves:
        g[h, z, y] = basis[:, 128 * h : 128 * h + 128]
    pl.semaphore_wait(barrier, NZ + NY + NX - 3 + 1)

    sends = []

    def copy(src, dst, ss, rs, dev):
        cp = pltpu.make_async_remote_copy(src, dst, ss, rs, device_id=dev)
        cp.start()
        sends.append(cp)
        return cp

    hi, lo = pl.ds(0, GA), pl.ds(GA, BLK - GA)
    cy, cz, cyz, czy = {}, {}, {}, {}
    for h in halves:
        k128 = pl.ds(128 * h, 128)
        for s in near:
            cz[h, s] = copy(basis.at[hi, k128], g.at[h, z, y, hi], s_gz.at[h, s], r_gz.at[h, s], at_z(s))
        for s in (2, 1, 3):
            cy[h, s] = copy(basis.at[lo, k128], g.at[h, z, y, lo], s_gy.at[h, s], r_gy.at[h, s], at_y(s))
        for t in (2, 1, 3):
            czy[h, 0, t] = copy(basis.at[hi, k128], g.at[h, z, y, hi], s_gzy.at[h, 0, t], r_gzy.at[h, 0, t], at_y(t))
    for h in halves:
        for s in (1, 3, 2):
            cy[h, s].wait_recv()
        for s in far:
            cyz[h, s] = copy(g.at[h, z, :, lo], g.at[h, z, :, lo], s_gyz.at[h, s], r_gyz.at[h, s], at_z(s))
        for s in near:
            cz[h, s].wait_recv()
            zs = (z + NZ - s) % NZ
            for t in (2, 1, 3):
                czy[h, s, t] = copy(
                    g.at[h, zs, y, hi], g.at[h, zs, y, hi], s_gzy.at[h, s, t], r_gzy.at[h, s, t], at_y(t)
                )

    def product(h, j):
        return jnp.dot(bt[h], av[j], preferred_element_type=F32)

    cx = {}
    for h in halves:
        for s in far:
            cyz[h, s].wait_recv()
        for s in (0, *near):
            for t in (1, 3, 2):
                czy[h, s, t].wait_recv()

        for i in range(NZ):
            bt[h, :, 256 * i : 256 * i + 256] = g[h, i].reshape(NY * BLK, 128).T
        if h == 0:
            for cp in loads:
                cp.wait()
        ck = []
        for i, s in enumerate(XS):
            part[h, i] = product(h, 2 * ((x + s) % NX) + 1 - k)
            ck.append(copy(part.at[h, i], rk.at[h, i], s_k.at[h, i], r_k.at[h, i], at_k()))
        for i, s in enumerate(XS):
            p = product(h, 2 * ((x + s) % NX) + k)
            ck[i].wait_recv()
            p = p + rk[h, i]
            if s:
                src, dst = (xs2.at[h], xr2.at[h]) if s == 2 else (xs1.at[h, i - 1], xr1.at[h, i - 1])
                src[...] = p.astype(src.dtype)
                cx[h, i] = copy(src, dst, s_x.at[h, i], r_x.at[h, i], at_x(s))
            else:
                own[h] = p
    csx, csk = {}, {}
    for h in halves:
        for i in (1, 2, 0):
            cx[h, i].wait_recv()
        total = (own[h] + xr2[h].astype(F32)) + (xr1[h, 0].astype(F32) + xr1[h, 1].astype(F32))
        st[h, r] = (total * (16384.0**-0.5)).astype(BF16)
        mine = st.at[h, r]
        for s in (2, 1, 3):
            csx[h, s] = copy(mine, mine, s_sx.at[h, s], r_sx.at[h, s], at_x(s))
        csk[h, 0] = copy(mine, mine, s_sk.at[h, 0], r_sk.at[h, 0], at_k())

    nb = BLK - IA
    cya, czb, cza, cyb = {}, {}, {}, {}
    for h in halves:

        def add(ja, jb, first):
            dims = (((1,), (1,)), ((), ()))
            for i in range(8):
                rows = pl.ds(256 * i, 256)
                v = lax.dot_general(av[ja, rows, :], st[h, ja], dims, preferred_element_type=F32)
                v += lax.dot_general(av[jb, rows, :], st[h, jb], dims, preferred_element_type=F32)
                if not first:
                    v += im[h, rows, :]
                im[h, rows, :] = v

        csk[h, 0].wait_recv()
        add(r, x * 2 + 1 - k, True)
        for s in (1, 3, 2):
            csx[h, s].wait_recv()
            j = 2 * ((x + NX - s) % NX) + k
            csk[h, s] = copy(st.at[h, j], st.at[h, j], s_sk.at[h, s], r_sk.at[h, s], at_k())
        for s in (1, 3, 2):
            csk[h, s].wait_recv()
            xq = (x + NX - s) % NX
            add(2 * xq + k, 2 * xq + 1 - k, False)
        v4 = im.reshape(2, NZ, NY, BLK, 128)
        for s in (2, 1, 3):
            sa[h, s] = v4[h, :, (y + s) % NY, :IA, :].astype(IDT)
            cya[h, s] = copy(sa.at[h, s], ya.at[h, s], s_ya.at[h, s], r_ya.at[h, s], at_y(s))
        for s in far:
            sb[h, s] = v4[h, (z + s) % NZ, :, IA:, :].astype(IDT)
            czb[h, s] = copy(sb.at[h, s], zb.at[h, s], s_zb.at[h, s], r_zb.at[h, s], at_z(s))
        ta[h] = v4[h, :, y, :IA, :]
        ub[h] = v4[h, z, :, IA:, :]
    for h in halves:
        for s in (1, 3, 2):
            cya[h, s].wait_recv()
        ta[h] = (ta[h] + ya[h, 1].astype(F32)) + (ya[h, 2].astype(F32) + ya[h, 3].astype(F32))
        for s in far:
            cza[h, s] = copy(ta.at[h, (z + s) % NZ], za.at[h, s], s_za.at[h, s], r_za.at[h, s], at_z(s))
        u = ub[h]
        for s in near:
            czb[h, s].wait_recv()
            u = u + zb[h, s].astype(F32)
        ub[h] = u
        for s in (2, 1, 3):
            cyb[h, s] = copy(ub.at[h, (y + s) % NY], yb.at[h, s], s_yb.at[h, s], r_yb.at[h, s], at_y(s))
    scale = 65536.0**-0.5
    for h in halves:
        low = ub[h, y]
        for s in (1, 3, 2):
            cyb[h, s].wait_recv()
            low = low + yb[h, s]
        high = ta[h, z]
        for s in near:
            cza[h, s].wait_recv()
            high = high + za[h, s]
        img_out[:IA, 128 * h : 128 * h + 128] = high * scale
        img_out[IA:, 128 * h : 128 * h + 128] = low * scale

    img = img_out[...]
    g0[...] = lax.dot_general(
        img, img, (((0,), (0,)), ((), ())),
        precision=lax.Precision.HIGHEST, preferred_element_type=F32,
    ) * (1.0 / 16384.0)
    half = pl.multiple_of(128 * k, 128)
    cp = copy(g0.at[pl.ds(pl.multiple_of(128 * (1 - k), 128), 128)], gk, s_q.at[0], r_q.at[0], at_k())
    cp.wait_recv()
    g1[...] = g0[pl.ds(half, 128), :] + gk[...]

    def rows8(xq, yq):
        return pl.ds(pl.multiple_of(32 * xq + 8 * yq, 8), 8)

    cps = []
    for s, t in sorted(shifts, key=lambda v: -min(v[0], NX - v[0]) - min(v[1], NY - v[1])):
        q = NY * s + t
        piece = g1.at[rows8((x + s) % NX, (y + t) % NY)]
        cps.append(copy(piece, gx.at[q], s_q.at[q], r_q.at[q], at_xy(s, t)))
    acc = g1[rows8(x, y), :]
    for (s, t), cp in zip(reversed(shifts), reversed(cps)):
        cp.wait_recv()
    for s, t in shifts:
        acc = acc + gx[NY * s + t]
    gz[z] = acc
    cps = []
    for s in far:
        cps.append(copy(gz.at[z], gz.at[z], s_q.at[15 + s], r_q.at[15 + s], at_z(s)))
    for cp in cps:
        cp.wait_recv()
    row8 = pl.ds(pl.multiple_of(half + 32 * x + 8 * y, 8), 8)
    gf[row8, :] = ((gz[0] + gz[1]) + (gz[2] + gz[3])) + ((gz[4] + gz[5]) + (gz[6] + gz[7]))
    cps = {}
    for s, t in sorted(shifts, key=lambda v: -min(v[0], NX - v[0]) - min(v[1], NY - v[1])):
        q = 23 + NY * s + t
        cps[s, t] = copy(gf.at[row8], gf.at[row8], s_q.at[q], r_q.at[q], at_xy(s, t))
    ckf = []
    for s in (0, 1, 3, 2):
        for t in range(NY):
            if s or t:
                cps[s, t].wait_recv()
        row32 = gf.at[pl.ds(pl.multiple_of(half + 32 * ((x + NX - s) % NX), 32), 32)]
        ckf.append(copy(row32, row32, s_q.at[39 + s], r_q.at[39 + s], at_k()))
    for cp in ckf:
        cp.wait_recv()
    gram_out[...] = gf[...]
    for cp in sends:
        cp.wait_send()


def image_and_gram(matrix, basis):
    dma = pltpu.SemaphoreType.DMA
    nb = BLK - IA
    sems = []
    for shape in (
        (2, NZ), (2, NZ, NY), (2, NY), (2, NZ),
        (2, 4), (2, 3), (2, 4), (2, 4),
        (2, NY), (2, NZ), (2, NZ), (2, NY), (43,),
    ):
        sems += [dma(shape), dma(shape)]
    return pl.pallas_call(
        kernel,
        out_shape=(
            jax.ShapeDtypeStruct((BLK, KC), F32),
            jax.ShapeDtypeStruct((KC, KC), F32),
        ),
        in_specs=[pl.BlockSpec(memory_space=pltpu.HBM)] * 2,
        out_specs=(pl.BlockSpec(memory_space=pltpu.VMEM), pl.BlockSpec(memory_space=pltpu.VMEM)),
        scratch_shapes=[
            pltpu.VMEM((8, 2048, 256), BF16),
            pltpu.VMEM((BLK, KC), BF16),
            pltpu.VMEM((2, NZ, NY, BLK, 128), BF16),
            pltpu.VMEM((2, 128, 2048), BF16),
            pltpu.VMEM((2, 4, 128, 256), F32),
            pltpu.VMEM((2, 4, 128, 256), F32),
            pltpu.VMEM((2, 128, 256), F32),
            pltpu.VMEM((2, 128, 256), XFAR),
            pltpu.VMEM((2, 2, 128, 256), XNEAR),
            pltpu.VMEM((2, 128, 256), XFAR),
            pltpu.VMEM((2, 2, 128, 256), XNEAR),
            pltpu.VMEM((2, 8, 128, 256), BF16),
            pltpu.VMEM((2, 2048, 128), F32),
            pltpu.VMEM((2, NY, NZ, IA, 128), IDT),
            pltpu.VMEM((2, NZ, NY, nb, 128), IDT),
            pltpu.VMEM((2, NY, NZ, IA, 128), IDT),
            pltpu.VMEM((2, NZ, NY, nb, 128), IDT),
            pltpu.VMEM((2, NZ, IA, 128), F32),
            pltpu.VMEM((2, NY, nb, 128), F32),
            pltpu.VMEM((2, NZ, IA, 128), F32),
            pltpu.VMEM((2, NY, nb, 128), F32),
            pltpu.VMEM((KC, KC), F32),
            pltpu.VMEM((128, KC), F32),
            pltpu.VMEM((128, KC), F32),
            pltpu.VMEM((NX * NY, 8, KC), F32),
            pltpu.VMEM((NZ, 8, KC), F32),
            pltpu.VMEM((KC, KC), F32),
            dma((9,)),
            *sems,
        ],
        compiler_params=pltpu.CompilerParams(
            collective_id=0, has_side_effects=True, vmem_limit_bytes=48 * 2**20
        ),
        cost_estimate=pl.CostEstimate(flops=2**33, bytes_accessed=2**23, transcendentals=0),
        name="image_and_gram",
    )(matrix, basis)


def factor(w, n):
    w = list(w)
    ng = len(w)
    row = lax.broadcasted_iota(jnp.int32, (8, n), 0)
    row1 = lax.broadcasted_iota(jnp.int32, (8, 128), 0)
    wide = lambda v: jnp.concatenate([v] * (n // 128), axis=1)
    out = []
    for g in range(ng):
        z = f = w[g]
        j0 = 8 * g
        dc = [jnp.broadcast_to(z[:, j0 + t : j0 + t + 1], (8, 128)) for t in range(8)]
        for t in range(0, 8, 2):
            u = t + 1
            p, q = dc[t], dc[u]
            a = jnp.broadcast_to(p[t : t + 1, :], (8, 128))
            b = jnp.broadcast_to(p[u : u + 1, :], (8, 128))
            c = jnp.broadcast_to(q[u : u + 1, :], (8, 128))
            det = a * c - b * b
            rdet = lax.rsqrt(det)
            r = rdet * rdet
            ar, br, cr = a * r, b * r, c * r
            for s in range(u + 1, 8):
                et = jnp.broadcast_to(dc[s][t : t + 1, :], (8, 128))
                eu = jnp.broadcast_to(dc[s][u : u + 1, :], (8, 128))
                nt, nu = cr * et - br * eu, ar * eu - br * et
                dc[s] = jnp.where(row1 == t, nt, jnp.where(row1 == u, nu, (dc[s] - p * nt) - q * nu))
            zt = jnp.broadcast_to(z[t : t + 1, :], (8, n))
            zu = jnp.broadcast_to(z[u : u + 1, :], (8, n))
            ra = lax.rsqrt(a)
            sa = a * ra
            ba = b * (ra * ra)
            rd = rdet * sa
            ft = zt * wide(ra)
            fu = (zu - wide(ba) * zt) * wide(rd)
            f = jnp.where(row == t, ft, jnp.where(row == u, fu, f))
            nt, nu = wide(cr) * zt - wide(br) * zu, wide(ar) * zu - wide(br) * zt
            z = jnp.where(row == t, nt, jnp.where(row == u, nu, (z - wide(p) * nt) - wide(q) * nu))
        out.append(f)
        for i in range(g + 1, ng):
            acc = w[i]
            for t in range(8):
                cc = jnp.broadcast_to(w[i][:, j0 + t : j0 + t + 1], (8, n))
                acc = acc - cc * jnp.broadcast_to(z[t : t + 1, :], (8, n))
            w[i] = acc
    return out

def tail(gram, image, ortho, tri):
    def dot(a, b, ca, cb):
        return lax.dot_general(a, b, (((ca,), (cb,)), ((), ())), precision=lax.Precision.HIGHEST, preferred_element_type=F32)

    rr = lax.broadcasted_iota(jnp.int32, (128, 128), 0)
    cc = lax.broadcasted_iota(jnp.int32, (128, 128), 1)
    eye = (rr == cc).astype(F32)
    up = cc >= rr
    lo, hi = slice(0, 128), slice(128, 256)
    diag = [gram[q, q] * eye for q in (lo, hi)]
    across = [jnp.sum(d, axis=0, keepdims=True) for d in diag]
    down = [lax.rsqrt(jnp.sum(d, axis=1, keepdims=True)) for d in diag]
    inv = [lax.rsqrt(d) for d in across]
    root = [d * v for d, v in zip(across, inv)]
    def groups(*blocks):
        m = jnp.concatenate(blocks, axis=1)
        return [m[8 * g : 8 * g + 8, :] for g in range(16)]

    w = groups(gram[lo, lo] * (down[0] * inv[0]), gram[lo, hi] * (down[0] * inv[1]), eye)
    o = jnp.concatenate(factor(w, 384), axis=0)
    u12 = o[:, hi]
    a22 = gram[hi, hi] * (down[1] * inv[1]) - dot(u12, u12, 0, 0)
    q1 = dot(image[:, lo] * inv[0], o[:, 256:], 1, 1)
    rest = image[:, hi] * inv[1] - dot(q1, u12, 1, 0)
    o2 = jnp.concatenate(factor(groups(a22, eye), 256), axis=0)
    ortho[:, lo] = q1
    ortho[:, hi] = dot(rest, o2[:, hi], 1, 1)
    tri[lo, lo] = jnp.where(up, o[:, lo] * root[0], 0.0)
    tri[lo, hi] = u12 * root[1]
    tri[hi, lo] = jnp.zeros((128, 128), F32)
    tri[hi, hi] = jnp.where(up, o2[:, lo] * root[1], 0.0)


def orthonormalise(image, gram):
    v = pl.BlockSpec(memory_space=pltpu.VMEM)
    return pl.pallas_call(
        tail,
        out_shape=(jax.ShapeDtypeStruct(image.shape, F32), jax.ShapeDtypeStruct(gram.shape, F32)),
        in_specs=[v, v],
        out_specs=(v, v),
        compiler_params=pltpu.CompilerParams(vmem_limit_bytes=16 * 2**20),
        name="orthonormalise",
    )(gram, image)


def body(matrix, basis):
    return orthonormalise(*image_and_gram(matrix, basis))


def solution(mesh):
    in_specs = (P("row", "col"), P(("row", "col"), None))
    out_specs = (P(("row", "col"), None), P())
    return jax.shard_map(body, mesh=mesh, in_specs=in_specs, out_specs=out_specs, check_vma=False)
```

```python
import jax
import jax.numpy as jnp
from jax import lax
from jax.experimental import pallas as pl
from jax.experimental.pallas import tpu as pltpu
from jax.sharding import PartitionSpec as P

F32 = jnp.float32
BF16 = jnp.bfloat16
NX, NY, NZ = 4, 4, 8
KC = 256
BLK = 64
GA = 48
IA = 48
ZPOS = (0, 1, 7, 2, 6, 3, 5, 4)
ZGROUPS = ((0, 5), (5, 8))
IDT = BF16
XS = (2, 1, 3, 0)
XFAR, XNEAR = BF16, F32


def kernel(
    a_hbm, b_hbm, img_out, gram_out,
    av, basis, g, bt, part, rk, own, xs2, xs1, xr2, xr1, st, im, sa, sb, ya, zb, ta, ub, za, yb,
    g0, gk, g1, gx, gz, gf,
    asem, s_gz, r_gz, s_gzy, r_gzy, s_gy, r_gy, s_gyz, r_gyz,
    s_k, r_k, s_x, r_x, s_sx, r_sx, s_sk, r_sk,
    s_ya, r_ya, s_zb, r_zb, s_za, r_za, s_yb, r_yb,
    s_q, r_q,
):
    r = lax.axis_index("row")
    c = lax.axis_index("col")
    x, k = r // 2, r % 2
    z, y = c // NY, c % NY

    def at_xy(s, t):
        return (((x + s) % NX) * 2 + k, z * NY + (y + t) % NY)

    def at_x(s):
        return at_xy(s, 0)

    def at_k():
        return (x * 2 + 1 - k, c)

    def at_y(s):
        return at_xy(0, s)

    def at_z(s):
        return (r, ((z + s) % NZ) * NY + y)

    shifts = [(s, t) for s in range(NX) for t in range(NY) if s or t]
    far = (4, 3, 5, 2, 6, 1, 7)
    near = (1, 7, 2, 6, 3, 5, 4)
    halves = range(2)

    first = pltpu.make_async_copy(b_hbm, basis, asem.at[8])
    first.start()
    loads = []
    for j in range(8):
        cp = pltpu.make_async_copy(a_hbm.at[:, pl.ds(256 * j, 256)], av.at[j], asem.at[j])
        cp.start()
        loads.append(cp)

    barrier = pltpu.get_barrier_semaphore()
    for s in far:
        pl.semaphore_signal(barrier, 1, device_id=at_z(s))
    for s in range(1, NY):
        pl.semaphore_signal(barrier, 1, device_id=at_y(s))
    for s in range(1, NX):
        pl.semaphore_signal(barrier, 1, device_id=at_x(s))
    pl.semaphore_signal(barrier, 1, device_id=at_k())
    first.wait()
    for h in halves:
        g[h, 0, y] = basis[:, 128 * h : 128 * h + 128]
    pl.semaphore_wait(barrier, NZ + NY + NX - 3 + 1)

    sends = []

    def copy(src, dst, ss, rs, dev):
        cp = pltpu.make_async_remote_copy(src, dst, ss, rs, device_id=dev)
        cp.start()
        sends.append(cp)
        return cp

    def drain(*keep):
        kept = [cp for group in keep for cp in group]
        for cp in sends:
            if all(cp is not other for other in kept):
                cp.wait_send()
        sends[:] = kept

    hi, lo = pl.ds(0, GA), pl.ds(GA, BLK - GA)
    cy, cz, cyz, czy = {}, {}, {}, {}
    for h in halves:
        k128 = pl.ds(128 * h, 128)
        for s in near:
            cz[h, s] = copy(
                basis.at[hi, k128], g.at[h, ZPOS.index(s), y, hi], s_gz.at[h, s], r_gz.at[h, s], at_z(s)
            )
        for s in (2, 1, 3):
            cy[h, s] = copy(basis.at[lo, k128], g.at[h, 0, y, lo], s_gy.at[h, s], r_gy.at[h, s], at_y(s))
    for h in halves:
        for s in (1, 3, 2):
            cy[h, s].wait_recv()
        for s in far:
            cyz[h, s] = copy(
                g.at[h, 0, :, lo], g.at[h, ZPOS.index(s), :, lo], s_gyz.at[h, s], r_gyz.at[h, s], at_z(s)
            )
        for q, (first, last) in enumerate(ZGROUPS):
            for s in ZPOS[first:last]:
                if s:
                    cz[h, s].wait_recv()
            blocks = g.at[h, pl.ds(first, last - first), y, hi]
            for t in (2, 1, 3):
                czy[h, q, t] = copy(blocks, blocks, s_gzy.at[h, q, t], r_gzy.at[h, q, t], at_y(t))

    def product(h, j):
        return jnp.dot(bt[h], av[j], preferred_element_type=F32)

    cx = {}
    for h in halves:
        for s in far:
            cyz[h, s].wait_recv()
        for q in range(len(ZGROUPS)):
            for t in (1, 3, 2):
                czy[h, q, t].wait_recv()

        for i, s in enumerate(ZPOS):
            at = pl.ds(pl.multiple_of(256 * ((z + NZ - s) % NZ), 256), 256)
            bt[h, :, at] = g[h, i].reshape(NY * BLK, 128).T
        if h == 0:
            for cp in loads:
                cp.wait()
        ck = []
        for i, s in enumerate(XS):
            part[h, i] = product(h, 2 * ((x + s) % NX) + 1 - k)
            ck.append(copy(part.at[h, i], rk.at[h, i], s_k.at[h, i], r_k.at[h, i], at_k()))
        for i, s in enumerate(XS):
            p = product(h, 2 * ((x + s) % NX) + k)
            ck[i].wait_recv()
            p = p + rk[h, i]
            if s:
                src, dst = (xs2.at[h], xr2.at[h]) if s == 2 else (xs1.at[h, i - 1], xr1.at[h, i - 1])
                src[...] = p.astype(src.dtype)
                cx[h, i] = copy(src, dst, s_x.at[h, i], r_x.at[h, i], at_x(s))
            else:
                own[h] = p
    drain(cx.values())
    csx, csk = {}, {}
    for h in halves:
        for i in (1, 2, 0):
            cx[h, i].wait_recv()
        total = (own[h] + xr2[h].astype(F32)) + (xr1[h, 0].astype(F32) + xr1[h, 1].astype(F32))
        st[h, r] = (total * (16384.0**-0.5)).astype(BF16)
        mine = st.at[h, r]
        for s in (2, 1, 3):
            csx[h, s] = copy(mine, mine, s_sx.at[h, s], r_sx.at[h, s], at_x(s))
        csk[h, 0] = copy(mine, mine, s_sk.at[h, 0], r_sk.at[h, 0], at_k())
    drain(csx.values(), csk.values())

    nb = BLK - IA
    cya, czb, cza, cyb = {}, {}, {}, {}
    for h in halves:

        def add(ja, jb, first):
            dims = (((1,), (1,)), ((), ()))
            for i in range(8):
                rows = pl.ds(256 * i, 256)
                v = lax.dot_general(av[ja, rows, :], st[h, ja], dims, preferred_element_type=F32)
                v += lax.dot_general(av[jb, rows, :], st[h, jb], dims, preferred_element_type=F32)
                if not first:
                    v += im[h, rows, :]
                im[h, rows, :] = v

        csk[h, 0].wait_recv()
        add(r, x * 2 + 1 - k, True)
        for s in (1, 3, 2):
            csx[h, s].wait_recv()
            j = 2 * ((x + NX - s) % NX) + k
            csk[h, s] = copy(st.at[h, j], st.at[h, j], s_sk.at[h, s], r_sk.at[h, s], at_k())
        for s in (1, 3, 2):
            csk[h, s].wait_recv()
            xq = (x + NX - s) % NX
            add(2 * xq + k, 2 * xq + 1 - k, False)
        v4 = im.reshape(2, NZ, NY, BLK, 128)
        for s in (2, 1, 3):
            sa[h, s] = v4[h, :, (y + s) % NY, :IA, :].astype(IDT)
            cya[h, s] = copy(sa.at[h, s], ya.at[h, s], s_ya.at[h, s], r_ya.at[h, s], at_y(s))
        for s in far:
            sb[h, s] = v4[h, (z + s) % NZ, :, IA:, :].astype(IDT)
            czb[h, s] = copy(sb.at[h, s], zb.at[h, s], s_zb.at[h, s], r_zb.at[h, s], at_z(s))
        ta[h] = v4[h, :, y, :IA, :]
        ub[h] = v4[h, z, :, IA:, :]
    drain(cya.values(), czb.values())
    for h in halves:
        for s in (1, 3, 2):
            cya[h, s].wait_recv()
        ta[h] = (ta[h] + ya[h, 1].astype(F32)) + (ya[h, 2].astype(F32) + ya[h, 3].astype(F32))
        for s in far:
            cza[h, s] = copy(ta.at[h, (z + s) % NZ], za.at[h, s], s_za.at[h, s], r_za.at[h, s], at_z(s))
        u = ub[h]
        for s in near:
            czb[h, s].wait_recv()
            u = u + zb[h, s].astype(F32)
        ub[h] = u
        for s in (2, 1, 3):
            cyb[h, s] = copy(ub.at[h, (y + s) % NY], yb.at[h, s], s_yb.at[h, s], r_yb.at[h, s], at_y(s))
    drain(cza.values(), cyb.values())
    scale = 65536.0**-0.5
    for h in halves:
        low = ub[h, y]
        for s in (1, 3, 2):
            cyb[h, s].wait_recv()
            low = low + yb[h, s]
        high = ta[h, z]
        for s in near:
            cza[h, s].wait_recv()
            high = high + za[h, s]
        img_out[:IA, 128 * h : 128 * h + 128] = high * scale
        img_out[IA:, 128 * h : 128 * h + 128] = low * scale

    img = img_out[...]
    g0[...] = lax.dot_general(
        img, img, (((0,), (0,)), ((), ())),
        precision=lax.Precision.HIGHEST, preferred_element_type=F32,
    ) * (1.0 / 16384.0)
    half = pl.multiple_of(128 * k, 128)
    cp = copy(g0.at[pl.ds(pl.multiple_of(128 * (1 - k), 128), 128)], gk, s_q.at[0], r_q.at[0], at_k())
    drain([cp])
    cp.wait_recv()
    g1[...] = g0[pl.ds(half, 128), :] + gk[...]

    def rows8(xq, yq):
        return pl.ds(pl.multiple_of(32 * xq + 8 * yq, 8), 8)

    cps = []
    for s, t in sorted(shifts, key=lambda v: -min(v[0], NX - v[0]) - min(v[1], NY - v[1])):
        q = NY * s + t
        piece = g1.at[rows8((x + s) % NX, (y + t) % NY)]
        cps.append(copy(piece, gx.at[q], s_q.at[q], r_q.at[q], at_xy(s, t)))
    acc = g1[rows8(x, y), :]
    drain(cps)
    for (s, t), cp in zip(reversed(shifts), reversed(cps)):
        cp.wait_recv()
    for s, t in shifts:
        acc = acc + gx[NY * s + t]
    gz[z] = acc
    cps = []
    for s in far:
        cps.append(copy(gz.at[z], gz.at[z], s_q.at[15 + s], r_q.at[15 + s], at_z(s)))
    drain(cps)
    for cp in cps:
        cp.wait_recv()
    row8 = pl.ds(pl.multiple_of(half + 32 * x + 8 * y, 8), 8)
    gf[row8, :] = ((gz[0] + gz[1]) + (gz[2] + gz[3])) + ((gz[4] + gz[5]) + (gz[6] + gz[7]))
    cps = {}
    for s, t in sorted(shifts, key=lambda v: -min(v[0], NX - v[0]) - min(v[1], NY - v[1])):
        q = 23 + NY * s + t
        cps[s, t] = copy(gf.at[row8], gf.at[row8], s_q.at[q], r_q.at[q], at_xy(s, t))
    drain(cps.values())
    ckf = []
    for s in (0, 1, 3, 2):
        for t in range(NY):
            if s or t:
                cps[s, t].wait_recv()
        row32 = gf.at[pl.ds(pl.multiple_of(half + 32 * ((x + NX - s) % NX), 32), 32)]
        ckf.append(copy(row32, row32, s_q.at[39 + s], r_q.at[39 + s], at_k()))
    for cp in ckf:
        cp.wait_recv()
    gram_out[...] = gf[...]
    drain()


def image_and_gram(matrix, basis):
    dma = pltpu.SemaphoreType.DMA
    nb = BLK - IA
    sems = []
    for shape in (
        (2, NZ), (2, 2, NY), (2, NY), (2, NZ),
        (2, 4), (2, 3), (2, 4), (2, 4),
        (2, NY), (2, NZ), (2, NZ), (2, NY), (43,),
    ):
        sems += [dma(shape), dma(shape)]
    return pl.pallas_call(
        kernel,
        out_shape=(
            jax.ShapeDtypeStruct((BLK, KC), F32),
            jax.ShapeDtypeStruct((KC, KC), F32),
        ),
        in_specs=[pl.BlockSpec(memory_space=pltpu.HBM)] * 2,
        out_specs=(pl.BlockSpec(memory_space=pltpu.VMEM), pl.BlockSpec(memory_space=pltpu.VMEM)),
        scratch_shapes=[
            pltpu.VMEM((8, 2048, 256), BF16),
            pltpu.VMEM((BLK, KC), BF16),
            pltpu.VMEM((2, NZ, NY, BLK, 128), BF16),
            pltpu.VMEM((2, 128, 2048), BF16),
            pltpu.VMEM((2, 4, 128, 256), F32),
            pltpu.VMEM((2, 4, 128, 256), F32),
            pltpu.VMEM((2, 128, 256), F32),
            pltpu.VMEM((2, 128, 256), XFAR),
            pltpu.VMEM((2, 2, 128, 256), XNEAR),
            pltpu.VMEM((2, 128, 256), XFAR),
            pltpu.VMEM((2, 2, 128, 256), XNEAR),
            pltpu.VMEM((2, 8, 128, 256), BF16),
            pltpu.VMEM((2, 2048, 128), F32),
            pltpu.VMEM((2, NY, NZ, IA, 128), IDT),
            pltpu.VMEM((2, NZ, NY, nb, 128), IDT),
            pltpu.VMEM((2, NY, NZ, IA, 128), IDT),
            pltpu.VMEM((2, NZ, NY, nb, 128), IDT),
            pltpu.VMEM((2, NZ, IA, 128), F32),
            pltpu.VMEM((2, NY, nb, 128), F32),
            pltpu.VMEM((2, NZ, IA, 128), F32),
            pltpu.VMEM((2, NY, nb, 128), F32),
            pltpu.VMEM((KC, KC), F32),
            pltpu.VMEM((128, KC), F32),
            pltpu.VMEM((128, KC), F32),
            pltpu.VMEM((NX * NY, 8, KC), F32),
            pltpu.VMEM((NZ, 8, KC), F32),
            pltpu.VMEM((KC, KC), F32),
            dma((9,)),
            *sems,
        ],
        compiler_params=pltpu.CompilerParams(
            collective_id=0, has_side_effects=True, vmem_limit_bytes=48 * 2**20
        ),
        cost_estimate=pl.CostEstimate(flops=2**33, bytes_accessed=2**23, transcendentals=0),
        name="image_and_gram",
    )(matrix, basis)


def factor(w, n):
    w = list(w)
    ng = len(w)
    row = lax.broadcasted_iota(jnp.int32, (8, n), 0)
    row1 = lax.broadcasted_iota(jnp.int32, (8, 128), 0)
    wide = lambda v: jnp.concatenate([v] * (n // 128), axis=1)
    out = []
    for g in range(ng):
        z = f = w[g]
        j0 = 8 * g
        dc = [jnp.broadcast_to(z[:, j0 + t : j0 + t + 1], (8, 128)) for t in range(8)]
        for t in range(0, 8, 2):
            u = t + 1
            p, q = dc[t], dc[u]
            a = jnp.broadcast_to(p[t : t + 1, :], (8, 128))
            b = jnp.broadcast_to(p[u : u + 1, :], (8, 128))
            c = jnp.broadcast_to(q[u : u + 1, :], (8, 128))
            det = a * c - b * b
            rdet = lax.rsqrt(det)
            r = rdet * rdet
            ar, br, cr = a * r, b * r, c * r
            for s in range(u + 1, 8):
                et = jnp.broadcast_to(dc[s][t : t + 1, :], (8, 128))
                eu = jnp.broadcast_to(dc[s][u : u + 1, :], (8, 128))
                nt, nu = cr * et - br * eu, ar * eu - br * et
                dc[s] = jnp.where(row1 == t, nt, jnp.where(row1 == u, nu, (dc[s] - p * nt) - q * nu))
            zt = jnp.broadcast_to(z[t : t + 1, :], (8, n))
            zu = jnp.broadcast_to(z[u : u + 1, :], (8, n))
            ra = lax.rsqrt(a)
            sa = a * ra
            ba = b * (ra * ra)
            rd = rdet * sa
            ft = zt * wide(ra)
            fu = (zu - wide(ba) * zt) * wide(rd)
            f = jnp.where(row == t, ft, jnp.where(row == u, fu, f))
            nt, nu = wide(cr) * zt - wide(br) * zu, wide(ar) * zu - wide(br) * zt
            z = jnp.where(row == t, nt, jnp.where(row == u, nu, (z - wide(p) * nt) - wide(q) * nu))
        out.append(f)
        for i in range(g + 1, ng):
            acc = w[i]
            for t in range(8):
                cc = jnp.broadcast_to(w[i][:, j0 + t : j0 + t + 1], (8, n))
                acc = acc - cc * jnp.broadcast_to(z[t : t + 1, :], (8, n))
            w[i] = acc
    return out

def tail(gram, image, ortho, tri):
    def dot(a, b, ca, cb):
        return lax.dot_general(a, b, (((ca,), (cb,)), ((), ())), precision=lax.Precision.HIGHEST, preferred_element_type=F32)

    rr = lax.broadcasted_iota(jnp.int32, (128, 128), 0)
    cc = lax.broadcasted_iota(jnp.int32, (128, 128), 1)
    eye = (rr == cc).astype(F32)
    up = cc >= rr
    lo, hi = slice(0, 128), slice(128, 256)
    diag = [gram[q, q] * eye for q in (lo, hi)]
    across = [jnp.sum(d, axis=0, keepdims=True) for d in diag]
    down = [lax.rsqrt(jnp.sum(d, axis=1, keepdims=True)) for d in diag]
    inv = [lax.rsqrt(d) for d in across]
    root = [d * v for d, v in zip(across, inv)]
    def groups(*blocks):
        m = jnp.concatenate(blocks, axis=1)
        return [m[8 * g : 8 * g + 8, :] for g in range(16)]

    w = groups(gram[lo, lo] * (down[0] * inv[0]), gram[lo, hi] * (down[0] * inv[1]), eye)
    o = jnp.concatenate(factor(w, 384), axis=0)
    u12 = o[:, hi]
    a22 = gram[hi, hi] * (down[1] * inv[1]) - dot(u12, u12, 0, 0)
    q1 = dot(image[:, lo] * inv[0], o[:, 256:], 1, 1)
    rest = image[:, hi] * inv[1] - dot(q1, u12, 1, 0)
    o2 = jnp.concatenate(factor(groups(a22, eye), 256), axis=0)
    ortho[:, lo] = q1
    ortho[:, hi] = dot(rest, o2[:, hi], 1, 1)
    tri[lo, lo] = jnp.where(up, o[:, lo] * root[0], 0.0)
    tri[lo, hi] = u12 * root[1]
    tri[hi, lo] = jnp.zeros((128, 128), F32)
    tri[hi, hi] = jnp.where(up, o2[:, lo] * root[1], 0.0)


def orthonormalise(image, gram):
    v = pl.BlockSpec(memory_space=pltpu.VMEM)
    return pl.pallas_call(
        tail,
        out_shape=(jax.ShapeDtypeStruct(image.shape, F32), jax.ShapeDtypeStruct(gram.shape, F32)),
        in_specs=[v, v],
        out_specs=(v, v),
        compiler_params=pltpu.CompilerParams(vmem_limit_bytes=16 * 2**20),
        name="orthonormalise",
    )(gram, image)


def body(matrix, basis):
    return orthonormalise(*image_and_gram(matrix, basis))


def solution(mesh):
    in_specs = (P("row", "col"), P(("row", "col"), None))
    out_specs = (P(("row", "col"), None), P())
    return jax.shard_map(body, mesh=mesh, in_specs=in_specs, out_specs=out_specs, check_vma=False)
```
